32 devices in a mesh: seq: 8 (over z, x), head: 4 (over y, core).
Axes of the slice: x: 2, y: 2, z: 4, core: 2. Of those that a mesh axis runs over, the one named last changes fastest.
Arguments:
- queries: bfloat16 [16384, 8192], P(('seq', 'head')), may hold values from -50 to 50
- keys: bfloat16 [16384, 1024], P(('seq', 'head')), may hold values from -6 to 6
- values: bfloat16 [16384, 1024], P(('seq', 'head')), may hold values from -15 to 15
- pattern: int32 [128, 16], replicated, may hold values from 0 to 126, as said below
- keep: int32 [128, 16], replicated, may hold values from 0 to 1, as said below
Outputs:
- attended: bfloat16 [16384, 8192], P(('seq', 'head'))
The draws below stay inside these ranges and needn't reach their ends.
Inputs may be any that keep to these rules, and one draw needn't show every extreme that they name: `pattern`: entry b of query block i's list is i - 1 for b = 0; for b >= 1 it is i - 2^b or i - 2^b with its lowest bit flipped; it is 0 wherever i < 2^b. `keep`: 0 wherever i < 2^b.
All inputs are finite; a program needn't handle non-finite values.
Results may differ from the reference program's by a relative error of at most 0.0049.
Values may be sent and summed in bfloat16 or wider, within the bound.
No kernel may reach another device: no remote copies, remote signals or barrier semaphores. Data moves between devices by JAX's collectives and lax.ppermute only.
A program may use at most 128 MiB of HBM per device.

```python
import math
import jax
import jax.numpy as jnp
from jax import lax

QUERY_HEADS = 64
KEY_VALUE_HEADS = 8
HEAD_SIZE = 128
BLOCK_TOKENS = 128
SLOTS = 16
SEQUENCE_TOKENS = 16384
SEQUENCE_BLOCKS = 128


def key_core(key):
    random_key_folder = jax.random.fold_in(key, 11)
    unscaled_keys = jnp.clip(jax.random.normal(random_key_folder, (SEQUENCE_TOKENS, KEY_VALUE_HEADS * HEAD_SIZE), jnp.float32), -6.0, 6.0)
    return unscaled_keys


def draw_keys(key, part):
    unscaled_keys = key_core(key)
    return unscaled_keys.astype(jnp.bfloat16)


def draw_queries(key, part):
    random_key_folder = jax.random.fold_in(key, 13)
    result = jnp.clip(jax.random.normal(random_key_folder, (SEQUENCE_TOKENS, QUERY_HEADS * HEAD_SIZE), jnp.float32) * 1.5, -9.0, 9.0)
    return result.astype(jnp.bfloat16)


def draw_pattern(key, part):
    block_index = jnp.arange(SEQUENCE_BLOCKS, dtype=jnp.int32)[:, None]
    level_index = jnp.arange(SLOTS, dtype=jnp.int32)[None, :]
    step_size = jnp.power(2, level_index).astype(jnp.int32)
    base_block = block_index - step_size
    flip_bits = jax.random.randint(jax.random.fold_in(key, 21), (SEQUENCE_BLOCKS, SLOTS), 0, 2, jnp.int32)
    flip_bits = jnp.where(level_index >= 1, flip_bits, 0)
    partner = base_block + flip_bits * (1 - 2 * (base_block % 2))
    return jnp.where(block_index >= step_size, partner, 0).astype(jnp.int32)


def draw_keep(key, part):
    block_index = jnp.arange(SEQUENCE_BLOCKS, dtype=jnp.int32)[:, None]
    level_index = jnp.arange(SLOTS, dtype=jnp.int32)[None, :]
    step_size = jnp.power(2, level_index).astype(jnp.int32)
    choose = jax.random.randint(jax.random.fold_in(key, 31), (SEQUENCE_BLOCKS, SLOTS), 0, 4, jnp.int32)
    return jnp.where((block_index >= step_size) & (choose > 0), 1, 0).astype(jnp.int32)


def level_of(rng, dims, cuts, least, top_value):
    gain, own = 1.0, jax.random.fold_in(rng, 6)
    for dim, blocks in cuts:
        draws = jnp.exp(jax.random.uniform(jax.random.fold_in(own, dim), (blocks,), jnp.float32, least / len(cuts), top_value / len(cuts)))
        gain = gain * jnp.repeat(draws, dims[dim] // blocks).reshape([-1 if axis == dim else 1 for axis in range(len(dims))])
    return gain


def gaussian(rng, shape, width, bound, shards=(), held_as=jnp.bfloat16):
    drawn = width * jax.random.normal(rng, shape, jnp.float32)
    if shards:
        drawn = drawn * level_of(rng, shape, shards, -0.22, 0.18)
    return jnp.clip(drawn, -bound, bound).astype(held_as)


def setup_inputs(seed: int = 0) -> dict:
    streams_of = jax.random.split(jax.random.key(seed), 6)
    return {
        "queries": draw_queries(jax.random.fold_in(streams_of[5], 71), 0),
        "keys": draw_keys(jax.random.fold_in(streams_of[5], 71), 0),
        "values": gaussian(streams_of[2], (SEQUENCE_TOKENS, KEY_VALUE_HEADS * HEAD_SIZE), 3.0, 15.0, ((0, 32),)),
        "pattern": draw_pattern(jax.random.fold_in(streams_of[5], 71), 0),
        "keep": draw_keep(jax.random.fold_in(streams_of[5], 71), 0),
    }


def reference(queries, keys, values, pattern, keep):
    group_width = QUERY_HEADS // KEY_VALUE_HEADS
    levels = (SEQUENCE_BLOCKS - 1).bit_length()
    score_scale = 1.0 / math.sqrt(HEAD_SIZE)
    key_block_rows = keys.reshape(SEQUENCE_BLOCKS, BLOCK_TOKENS, KEY_VALUE_HEADS, HEAD_SIZE)
    value_block_rows = values.reshape(SEQUENCE_BLOCKS, BLOCK_TOKENS, KEY_VALUE_HEADS, HEAD_SIZE)
    query_block_rows = queries.reshape(SEQUENCE_BLOCKS, BLOCK_TOKENS, KEY_VALUE_HEADS, group_width, HEAD_SIZE)
    causal = jnp.arange(BLOCK_TOKENS)[:, None] >= jnp.arange(BLOCK_TOKENS)[None, :]
    diag_slot = jnp.arange(levels + 1) == 0

    def block_attend(block_index):
        slot_blocks = pattern[block_index, :levels]
        key_sets = jnp.concatenate([key_block_rows[block_index][None], key_block_rows[slot_blocks]], 0).astype(jnp.float32)
        value_sets = jnp.concatenate([value_block_rows[block_index][None], value_block_rows[slot_blocks]], 0).astype(jnp.float32)
        query_rows = query_block_rows[block_index].astype(jnp.float32)
        scores = jnp.einsum('qgrd,lpgd->grqlp', query_rows, key_sets) * score_scale
        live_slots = jnp.concatenate([jnp.ones((1,), jnp.int32), keep[block_index, :levels]]) > 0
        allowed = jnp.where(diag_slot[None, :, None], causal[:, None, :], live_slots[None, :, None])
        scores = jnp.where(allowed, scores, -1e+30)
        peak = lax.optimization_barrier(jnp.max(scores, axis=(3, 4), keepdims=True))
        expo = jnp.exp(scores - peak)
        weights = (expo / lax.optimization_barrier(jnp.sum(expo, axis=(3, 4), keepdims=True))).astype(jnp.bfloat16)
        weights = lax.optimization_barrier(weights).astype(jnp.float32)
        result = jnp.einsum('grqlp,lpgd->qgrd', weights, value_sets)
        return result.astype(jnp.bfloat16).reshape(BLOCK_TOKENS, QUERY_HEADS * HEAD_SIZE)
    gathered = lax.map(block_attend, jnp.arange(SEQUENCE_BLOCKS, dtype=jnp.int32))
    return gathered.reshape(SEQUENCE_BLOCKS * BLOCK_TOKENS, QUERY_HEADS * HEAD_SIZE)
```

```python
import functools
import math

import jax
import jax.numpy as jnp
from jax import lax
from jax.experimental import pallas as pl
from jax.experimental.pallas import tpu as pltpu
from jax.sharding import PartitionSpec as P

QUERY_HEADS = 64
KEY_VALUE_HEADS = 8
HEAD_SIZE = 128
BLOCK_TOKENS = 128
GROUP = QUERY_HEADS // KEY_VALUE_HEADS
AXES = ("seq", "head")
CHUNKS = (4, 4)
ROW_HEADS = 2
MASKED = -1e30


def attend_kernel(
    levels, blocks, sources, place_ref, pattern_ref, keep_ref, q_ref, *refs
):
    count = len(sources)
    k_refs, v_refs = refs[:count], refs[count : 2 * count]
    out_ref = refs[-1]
    block = pl.program_id(1)
    first = place_ref[0] * blocks
    row = first + block

    def pick(source, local):
        local = jnp.clip(local, 0, blocks - 1)
        rows = pl.ds(pl.multiple_of(local * BLOCK_TOKENS, BLOCK_TOKENS), BLOCK_TOKENS)
        return k_refs[source][rows, :], v_refs[source][rows, :]

    k_parts, v_parts = [], []
    own_k, own_v = pick(0, block)
    k_parts.append(own_k)
    v_parts.append(own_v)
    biases = []
    for level in range(levels):
        span = 2**level
        named = pattern_ref[row, level]
        if span < blocks:
            local = named - first
            near_k, near_v = pick(0, local)
            far_k, far_v = pick(sources.index(1), local + blocks)
            k_parts.append(jnp.where(local >= 0, near_k, far_k))
            v_parts.append(jnp.where(local >= 0, near_v, far_v))
        else:
            shift = span // blocks
            part_k, part_v = pick(sources.index(shift), named - first + shift * blocks)
            k_parts.append(part_k)
            v_parts.append(part_v)
        bias = jnp.where(keep_ref[row, level] > 0, 0.0, MASKED).astype(jnp.float32)
        biases.append(jnp.full((1, BLOCK_TOKENS), bias, jnp.float32))
    k_all = jnp.concatenate(k_parts, 0)
    v_all = jnp.concatenate(v_parts, 0)
    v_ones = jnp.concatenate([v_all, jnp.ones_like(v_all)], 1)
    bias_row = jnp.concatenate(biases, 1)
    rows = ROW_HEADS * BLOCK_TOKENS
    token = lax.broadcasted_iota(jnp.int32, (rows, BLOCK_TOKENS), 0) % BLOCK_TOKENS
    other = lax.broadcasted_iota(jnp.int32, (rows, BLOCK_TOKENS), 1)
    causal = token >= other
    scale = math.log2(math.e) / math.sqrt(HEAD_SIZE)

    def scores_of(step):
        heads = range(step * ROW_HEADS, (step + 1) * ROW_HEADS)
        q = jnp.concatenate(
            [q_ref[:, h * HEAD_SIZE : (h + 1) * HEAD_SIZE] for h in heads], 0
        )
        return lax.dot_general(
            q, k_all, (((1,), (1,)), ((), ())), preferred_element_type=jnp.float32
        )

    steps = GROUP // ROW_HEADS
    ahead = scores_of(0)
    for step in range(steps):
        scores = ahead
        if step + 1 < steps:
            ahead = scores_of(step + 1)
        diag = jnp.where(causal, scores[:, :BLOCK_TOKENS], MASKED)
        rest = scores[:, BLOCK_TOKENS:] + bias_row
        scores = jnp.concatenate([diag, rest], 1)
        peak = jnp.max(scores, axis=1, keepdims=True)
        weights = jnp.exp2((scores - peak) * scale).astype(jnp.bfloat16)
        sums = jnp.dot(weights, v_ones, preferred_element_type=jnp.float32)
        result = (sums[:, :HEAD_SIZE] / sums[:, HEAD_SIZE:]).astype(jnp.bfloat16)
        for part in range(ROW_HEADS):
            h = step * ROW_HEADS + part
            out_ref[:, h * HEAD_SIZE : (h + 1) * HEAD_SIZE] = result[
                part * BLOCK_TOKENS : (part + 1) * BLOCK_TOKENS
            ]


def attend_chunk(queries, held, sources, place, pattern, keep, first_head, heads, total, out):
    rows, width = queries.shape
    blocks = rows // BLOCK_TOKENS
    levels = (blocks * total - 1).bit_length()
    group_width = GROUP * HEAD_SIZE

    def q_index(head, block, *_):
        return block, first_head + head

    in_specs = [pl.BlockSpec((BLOCK_TOKENS, group_width), q_index)]
    operands = [queries]
    for offset in (0, heads):
        for source in sources:
            in_specs.append(
                pl.BlockSpec((rows, HEAD_SIZE), lambda head, block, *_, o=offset: (0, o + head))
            )
            operands.append(held[source])
    aliases = {}
    if out is not None:
        in_specs.append(pl.BlockSpec(memory_space=pl.ANY))
        aliases = {3 + len(operands): 0}
        operands.append(out)
    flops = 4 * rows * heads * GROUP * (levels + 1) * BLOCK_TOKENS * HEAD_SIZE
    return pl.pallas_call(
        functools.partial(attend_kernel, levels, blocks, sources),
        grid_spec=pltpu.PrefetchScalarGridSpec(
            num_scalar_prefetch=3,
            grid=(heads, blocks),
            in_specs=in_specs,
            out_specs=pl.BlockSpec((BLOCK_TOKENS, group_width), q_index),
        ),
        out_shape=jax.ShapeDtypeStruct((rows, width), jnp.bfloat16),
        input_output_aliases=aliases,
        compiler_params=pltpu.CompilerParams(vmem_limit_bytes=48 * 2**20),
        cost_estimate=pl.CostEstimate(
            flops=flops,
            bytes_accessed=4 * rows * heads * GROUP * HEAD_SIZE,
            transcendentals=flops // (4 * HEAD_SIZE),
        ),
    )(place, pattern, keep, *operands)


def fetch(kv, place, total):
    held = {0: kv}
    stride = max(total // 4, 1)
    up = [(p, p + stride) for p in range(total - stride)]
    held[stride] = lax.ppermute(kv, AXES, up)
    if 2 * stride < total:
        held[2 * stride] = lax.ppermute(held[stride], AXES, [(s, t) for s, t in up if s >= stride])
    distance = stride // 2
    while distance:
        sent = jnp.where((place & distance) > 0, held[2 * distance], kv)
        held[distance] = lax.ppermute(sent, AXES, [(p, p ^ distance) for p in range(total)])
        distance //= 2
    return held


def body(queries, keys, values, pattern, keep):
    total = lax.axis_size(AXES)
    place = lax.axis_index(AXES).astype(jnp.int32)
    sources = tuple([0] + [2**b for b in range(total.bit_length() - 1)])
    helds, first = [], 0
    for heads in CHUNKS:
        columns = slice(first * HEAD_SIZE, (first + heads) * HEAD_SIZE)
        kv = jnp.concatenate([keys[:, columns], values[:, columns]], 1)
        helds.append((first, heads, fetch(kv, place, total)))
        first += heads
    out = None
    for first, heads, held in helds:
        out = attend_chunk(
            queries, held, sources, place.reshape(1), pattern, keep, first, heads, total, out
        )
    return out


def solution(mesh):
    return jax.shard_map(
        body,
        mesh=mesh,
        in_specs=(P(AXES, None), P(AXES, None), P(AXES, None), P(), P()),
        out_specs=P(AXES, None),
        check_vma=False,
    )
```

```python
import functools
import math

import jax
import jax.numpy as jnp
from jax import lax
from jax.experimental import pallas as pl
from jax.experimental.pallas import tpu as pltpu
from jax.sharding import PartitionSpec as P

QUERY_HEADS = 64
KEY_VALUE_HEADS = 8
HEAD_SIZE = 128
BLOCK_TOKENS = 128
GROUP = QUERY_HEADS // KEY_VALUE_HEADS
AXES = ("seq", "head")
CHUNKS = (2, 2, 2, 2)
ROW_HEADS = 2
MASKED = -1e30


def attend_kernel(
    levels, blocks, sources, place_ref, pattern_ref, keep_ref, q_ref, *refs
):
    count = len(sources)
    k_refs, v_refs = refs[:count], refs[count : 2 * count]
    out_ref = refs[-1]
    block = pl.program_id(1)
    first = place_ref[0] * blocks
    row = first + block

    def pick(source, local):
        local = jnp.clip(local, 0, blocks - 1)
        rows = pl.ds(pl.multiple_of(local * BLOCK_TOKENS, BLOCK_TOKENS), BLOCK_TOKENS)
        return k_refs[source][rows, :], v_refs[source][rows, :]

    k_parts, v_parts = [], []
    own_k, own_v = pick(0, block)
    k_parts.append(own_k)
    v_parts.append(own_v)
    biases = []
    for level in range(levels):
        span = 2**level
        named = pattern_ref[row, level]
        if span < blocks:
            local = named - first
            near_k, near_v = pick(0, local)
            far_k, far_v = pick(sources.index(1), local + blocks)
            k_parts.append(jnp.where(local >= 0, near_k, far_k))
            v_parts.append(jnp.where(local >= 0, near_v, far_v))
        else:
            shift = span // blocks
            part_k, part_v = pick(sources.index(shift), named - first + shift * blocks)
            k_parts.append(part_k)
            v_parts.append(part_v)
        bias = jnp.where(keep_ref[row, level] > 0, 0.0, MASKED).astype(jnp.float32)
        biases.append(jnp.full((1, BLOCK_TOKENS), bias, jnp.float32))
    k_all = jnp.concatenate(k_parts, 0)
    v_all = jnp.concatenate(v_parts, 0)
    v_ones = jnp.concatenate([v_all, jnp.ones_like(v_all)], 1)
    bias_row = jnp.concatenate(biases, 1)
    rows = ROW_HEADS * BLOCK_TOKENS
    token = lax.broadcasted_iota(jnp.int32, (rows, BLOCK_TOKENS), 0) % BLOCK_TOKENS
    other = lax.broadcasted_iota(jnp.int32, (rows, BLOCK_TOKENS), 1)
    causal = token >= other
    scale = math.log2(math.e) / math.sqrt(HEAD_SIZE)

    def scores_of(step):
        heads = range(step * ROW_HEADS, (step + 1) * ROW_HEADS)
        q = jnp.concatenate(
            [q_ref[:, h * HEAD_SIZE : (h + 1) * HEAD_SIZE] for h in heads], 0
        )
        return lax.dot_general(
            q, k_all, (((1,), (1,)), ((), ())), preferred_element_type=jnp.float32
        )

    steps = GROUP // ROW_HEADS
    ahead = scores_of(0)
    for step in range(steps):
        scores = ahead
        if step + 1 < steps:
            ahead = scores_of(step + 1)
        diag = jnp.where(causal, scores[:, :BLOCK_TOKENS], MASKED)
        rest = scores[:, BLOCK_TOKENS:] + bias_row
        scores = jnp.concatenate([diag, rest], 1)
        peak = jnp.max(scores, axis=1, keepdims=True)
        weights = jnp.exp2((scores - peak) * scale).astype(jnp.bfloat16)
        sums = jnp.dot(weights, v_ones, preferred_element_type=jnp.float32)
        result = (sums[:, :HEAD_SIZE] / sums[:, HEAD_SIZE:]).astype(jnp.bfloat16)
        for part in range(ROW_HEADS):
            h = step * ROW_HEADS + part
            out_ref[:, h * HEAD_SIZE : (h + 1) * HEAD_SIZE] = result[
                part * BLOCK_TOKENS : (part + 1) * BLOCK_TOKENS
            ]


def attend_chunk(queries, held, sources, slots, pattern, keep, first_head, heads, total, out):
    rows, width = queries.shape
    blocks = rows // BLOCK_TOKENS
    levels = (blocks * total - 1).bit_length()
    group_width = GROUP * HEAD_SIZE

    def q_index(head, block, *_):
        return block, first_head + head

    def kv_index(place, offset, head, block, slots_ref, *_):
        return slots_ref[1 + place], 0, offset + head

    in_specs = [pl.BlockSpec((BLOCK_TOKENS, group_width), q_index)]
    operands = [queries]
    for offset in (0, heads):
        for place, source in enumerate(sources):
            in_specs.append(
                pl.BlockSpec((None, rows, HEAD_SIZE), functools.partial(kv_index, place, offset))
            )
            operands.append(held[source])
    aliases = {}
    if out is not None:
        in_specs.append(pl.BlockSpec(memory_space=pl.ANY))
        aliases = {3 + len(operands): 0}
        operands.append(out)
    flops = 4 * rows * heads * GROUP * (levels + 1) * BLOCK_TOKENS * HEAD_SIZE
    return pl.pallas_call(
        functools.partial(attend_kernel, levels, blocks, sources),
        grid_spec=pltpu.PrefetchScalarGridSpec(
            num_scalar_prefetch=3,
            grid=(heads, blocks),
            in_specs=in_specs,
            out_specs=pl.BlockSpec((BLOCK_TOKENS, group_width), q_index),
        ),
        out_shape=jax.ShapeDtypeStruct((rows, width), jnp.bfloat16),
        input_output_aliases=aliases,
        compiler_params=pltpu.CompilerParams(vmem_limit_bytes=48 * 2**20),
        cost_estimate=pl.CostEstimate(
            flops=flops,
            bytes_accessed=4 * rows * heads * GROUP * HEAD_SIZE,
            transcendentals=flops // (4 * HEAD_SIZE),
        ),
    )(slots, pattern, keep, *operands)


def slot_indices(place, total):
    stride = max(total // 4, 1)
    index = {0: 0}
    for hops in (1, 2):
        index[hops * stride] = jnp.clip(place // stride - hops, 0, total // stride - 1)
    distance = stride // 2
    while distance:
        index[distance] = jnp.where((place & distance) > 0, 0, 1)
        distance //= 2
    return index


def fetch(kv, place, total, index):
    stride = max(total // 4, 1)
    groups = [[r + stride * k for k in range(total // stride)] for r in range(stride)]
    column = lax.all_gather(kv, AXES, axis_index_groups=groups)
    held = {0: kv[None], stride: column, 2 * stride: column}
    distance = stride // 2
    while distance:
        farther = lax.dynamic_index_in_dim(
            held[2 * distance], index[2 * distance], 0, keepdims=False
        )
        sent = jnp.where((place & distance) > 0, farther, kv)
        groups = [[p, p ^ distance] for p in range(total) if not p & distance]
        held[distance] = lax.all_gather(sent, AXES, axis_index_groups=groups)
        distance //= 2
    return held


def body(queries, keys, values, pattern, keep):
    total = lax.axis_size(AXES)
    place = lax.axis_index(AXES).astype(jnp.int32)
    sources = tuple([0] + [2**b for b in range(total.bit_length() - 1)])
    index = slot_indices(place, total)
    slots = jnp.stack([place] + [jnp.asarray(index[s], jnp.int32) for s in sources])
    helds, first = [], 0
    for heads in CHUNKS:
        columns = slice(first * HEAD_SIZE, (first + heads) * HEAD_SIZE)
        kv = jnp.concatenate([keys[:, columns], values[:, columns]], 1)
        helds.append((first, heads, fetch(kv, place, total, index)))
        first += heads
    out = None
    for first, heads, held in helds:
        out = attend_chunk(
            queries, held, sources, slots, pattern, keep, first, heads, total, out
        )
    return out


def solution(mesh):
    return jax.shard_map(
        body,
        mesh=mesh,
        in_specs=(P(AXES, None), P(AXES, None), P(AXES, None), P(), P()),
        out_specs=P(AXES, None),
        check_vma=False,
    )
```

```python
import functools
import math

import jax
import jax.numpy as jnp
from jax import lax
from jax.experimental import pallas as pl
from jax.experimental.pallas import tpu as pltpu
from jax.sharding import PartitionSpec as P

QUERY_HEADS = 64
KEY_VALUE_HEADS = 8
HEAD_SIZE = 128
BLOCK_TOKENS = 128
GROUP = QUERY_HEADS // KEY_VALUE_HEADS
AXES = ("seq", "head")
CHUNKS = (2, 2, 2, 2)
ROW_HEADS = 4
MASKED = -1e30
SCALE = math.log2(math.e) / math.sqrt(HEAD_SIZE)
LEAST_SUM = 1e-25
GREATEST_SUM = 1e30


def attend_kernel(levels, blocks, sources, place_ref, pattern_ref, keep_ref, q_ref, *refs):
    count = len(sources)
    k_refs, v_refs = refs[:count], refs[count : 2 * count]
    out_ref, token_ref = refs[-3:-1]
    bad_ref = refs[-1]
    first = place_ref[0] * blocks

    def pick(source, local):
        local = jnp.clip(local, 0, blocks - 1)
        rows = pl.ds(pl.multiple_of(local * BLOCK_TOKENS, BLOCK_TOKENS), BLOCK_TOKENS)
        return k_refs[source][rows, :], v_refs[source][rows, :]

    def gather(block):
        k_part, v_part = pick(0, block)
        ones = jnp.ones_like(v_part)
        k_parts, v_parts, lives = [k_part], [jnp.concatenate([v_part, ones], 1)], []
        for level in range(levels):
            span = 2**level
            named = pattern_ref[first + block, level]
            if span < blocks:
                local = named - first
                near_k, near_v = pick(0, local)
                far_k, far_v = pick(sources.index(1), local + blocks)
                k_part = jnp.where(local >= 0, near_k, far_k)
                v_part = jnp.where(local >= 0, near_v, far_v)
            else:
                shift = span // blocks
                k_part, v_part = pick(sources.index(shift), named - first + shift * blocks)
            live = keep_ref[first + block, level] > 0
            factor = jnp.where(live, 1.0, 0.0).astype(jnp.bfloat16)
            k_parts.append(k_part * factor)
            v_parts.append(jnp.concatenate([v_part * factor, ones * factor], 1))
            lives.append(live)
        return jnp.concatenate(k_parts, 0), jnp.concatenate(v_parts, 0), lives

    def query_rows(block, heads):
        rows = pl.ds(pl.multiple_of(block * BLOCK_TOKENS, BLOCK_TOKENS), BLOCK_TOKENS)
        return jnp.concatenate(
            [q_ref[rows, h * HEAD_SIZE : (h + 1) * HEAD_SIZE] for h in heads], 0
        )

    def score(q, k):
        return lax.dot_general(
            q, k, (((1,), (1,)), ((), ())), preferred_element_type=jnp.float32
        )

    def store(block, heads, sums):
        result = (sums[:, :HEAD_SIZE] / sums[:, HEAD_SIZE:]).astype(jnp.bfloat16)
        rows = pl.ds(pl.multiple_of(block * BLOCK_TOKENS, BLOCK_TOKENS), BLOCK_TOKENS)
        for part, h in enumerate(heads):
            out_ref[rows, h * HEAD_SIZE : (h + 1) * HEAD_SIZE] = result[
                part * BLOCK_TOKENS : (part + 1) * BLOCK_TOKENS
            ]

    def causal_of(heads):
        shape = (heads * BLOCK_TOKENS, BLOCK_TOKENS)
        token = lax.broadcasted_iota(jnp.int32, shape, 0) % BLOCK_TOKENS
        return token >= lax.broadcasted_iota(jnp.int32, shape, 1)

    def quick(block, bad):
        k, v, _ = gather(block)
        steps = [range(s, s + ROW_HEADS) for s in range(0, GROUP, ROW_HEADS)]
        causal = causal_of(ROW_HEADS)
        ahead = score(query_rows(block, steps[0]), k)
        for at, heads in enumerate(steps):
            scores = ahead
            if at + 1 < len(steps):
                ahead = score(query_rows(block, steps[at + 1]), k)
            weights = jnp.exp2(scores * SCALE)
            diag = jnp.where(causal, weights[:, :BLOCK_TOKENS], 0.0)
            weights = jnp.concatenate([diag, weights[:, BLOCK_TOKENS:]], 1)
            sums = jnp.dot(weights.astype(jnp.bfloat16), v, preferred_element_type=jnp.float32)
            total = sums[:, HEAD_SIZE:]
            fine = (total > LEAST_SUM) & (total < GREATEST_SUM)
            flags = jnp.where(fine, 0.0, 1.0).reshape(-1, 8, HEAD_SIZE)
            bad = jnp.maximum(bad, jnp.max(flags, axis=0))
            store(block, heads, sums)
        return bad

    def careful(block):
        k, v, lives = gather(block)
        bias = jnp.concatenate(
            [
                jnp.full((1, BLOCK_TOKENS), jnp.where(live, 0.0, MASKED), jnp.float32)
                for live in lives
            ],
            1,
        )
        causal = causal_of(1)
        for h in range(GROUP):
            scores = score(query_rows(block, [h]), k)
            diag = jnp.where(causal, scores[:, :BLOCK_TOKENS], MASKED)
            scores = jnp.concatenate([diag, scores[:, BLOCK_TOKENS:] + bias], 1)
            peak = jnp.max(scores, axis=1, keepdims=True)
            weights = jnp.exp2((scores - peak) * SCALE).astype(jnp.bfloat16)
            store(block, [h], jnp.dot(weights, v, preferred_element_type=jnp.float32))

    bad_ref[...] = lax.fori_loop(0, blocks, quick, jnp.zeros((8, HEAD_SIZE), jnp.float32))
    token_ref[0] = 0

    @pl.when(jnp.max(bad_ref[...]) > 0.0)
    def _():
        pl.loop(0, blocks)(careful)


def attend_chunk(queries, held, sources, place, pattern, keep, first_head, heads, total, out):
    rows, width = queries.shape
    blocks = rows // BLOCK_TOKENS
    levels = (blocks * total - 1).bit_length()
    group_width = GROUP * HEAD_SIZE

    def q_index(head, *_):
        return 0, first_head + head

    in_specs = [pl.BlockSpec((rows, group_width), q_index)]
    operands = [queries]
    for offset in (0, heads):
        for source in sources:
            in_specs.append(
                pl.BlockSpec((rows, HEAD_SIZE), lambda head, *_, o=offset: (0, o + head))
            )
            operands.append(held[source])
    aliases = {}
    if out is not None:
        in_specs.append(pl.BlockSpec(memory_space=pl.ANY))
        aliases = {3 + len(operands): 0}
        operands.append(out)
    flops = 4 * rows * heads * GROUP * (levels + 1) * BLOCK_TOKENS * HEAD_SIZE
    return pl.pallas_call(
        functools.partial(attend_kernel, levels, blocks, sources),
        grid_spec=pltpu.PrefetchScalarGridSpec(
            num_scalar_prefetch=3,
            grid=(heads,),
            in_specs=in_specs,
            out_specs=[
                pl.BlockSpec((rows, group_width), q_index),
                pl.BlockSpec(memory_space=pltpu.SMEM),
            ],
            scratch_shapes=[pltpu.VMEM((8, HEAD_SIZE), jnp.float32)],
        ),
        out_shape=[
            jax.ShapeDtypeStruct((rows, width), jnp.bfloat16),
            jax.ShapeDtypeStruct((1,), jnp.int32),
        ],
        input_output_aliases=aliases,
        compiler_params=pltpu.CompilerParams(vmem_limit_bytes=44 * 2**20),
        cost_estimate=pl.CostEstimate(
            flops=1,
            bytes_accessed=1,
            transcendentals=1,
        ),
    )(place, pattern, keep, *operands)


def zero_after(*others):
    total = jnp.int32(0)
    for other in others:
        if jnp.issubdtype(other.dtype, jnp.integer):
            total += other.reshape(-1)[0]
        else:
            corner = other[0, 0].astype(jnp.float32)
            total += (corner != corner).astype(jnp.int32)
    return total


def body(queries, keys, values, pattern, keep):
    total = lax.axis_size(AXES)
    place = lax.axis_index(AXES).astype(jnp.int32)
    sources = tuple([0] + [2**b for b in range(total.bit_length() - 1)])
    stride = max(total // 4, 1)
    up = [(p, p + stride) for p in range(total - stride)]
    up_far = [(s, t) for s, t in up if s >= stride]
    chunks = range(len(CHUNKS))
    firsts = [sum(CHUNKS[:c]) for c in chunks]
    held = []
    for first, heads in zip(firsts, CHUNKS):
        columns = slice(first * HEAD_SIZE, (first + heads) * HEAD_SIZE)
        held.append({0: jnp.concatenate([keys[:, columns], values[:, columns]], 1)})

    def climb(chunk):
        held[chunk][stride] = lax.ppermute(held[chunk][0], AXES, up)

    def climb_again(chunk):
        held[chunk][2 * stride] = lax.ppermute(held[chunk][stride], AXES, up_far)

    def swap(chunk, distance, *others):
        mine = held[chunk]
        upper = (place & distance) > zero_after(*others)
        sent = jnp.where(upper, mine[2 * distance], mine[0])
        mine[distance] = lax.ppermute(sent, AXES, [(p, p ^ distance) for p in range(total)])

    state = [None, None]

    def attend(chunk):
        state[:] = attend_chunk(
            queries,
            held[chunk],
            sources,
            place.reshape(1),
            pattern,
            keep,
            firsts[chunk],
            CHUNKS[chunk],
            total,
            state[0],
        )

    for chunk in chunks:
        climb(chunk)
    for chunk in chunks:
        climb_again(chunk)
    distances = [stride >> k for k in range(1, stride.bit_length())]
    for chunk in chunks[:-1]:
        for distance in distances:
            early = chunk == chunks[-2] and distance == distances[1]
            swap(chunk, distance, *([]))
    attend(0)
    for distance in distances:
        others = []
        if distance == distances[1]:
            others = [state[1]]
        if distance == distances[-1]:
            attend(1)
            others = [state[1]]
        swap(chunks[-1], distance, *others)
    attend(2)
    attend(3)
    return state[0]


def solution(mesh):
    return jax.shard_map(
        body,
        mesh=mesh,
        in_specs=(P(AXES, None), P(AXES, None), P(AXES, None), P(), P()),
        out_specs=P(AXES, None),
        check_vma=False,
    )
```

```python
import functools
import math

import jax
import jax.numpy as jnp
from jax import lax
from jax.experimental import pallas as pl
from jax.experimental.pallas import tpu as pltpu
from jax.sharding import PartitionSpec as P

QUERY_HEADS = 64
KEY_VALUE_HEADS = 8
HEAD_SIZE = 128
BLOCK_TOKENS = 128
GROUP = QUERY_HEADS // KEY_VALUE_HEADS
AXES = ("seq", "head")
CHUNKS = (2, 2, 2, 2)
ROW_HEADS = 4
TILE_KEYS = 256
STEP_BLOCKS = 2
MASKED = -1e30
SCALE = math.log2(math.e) / math.sqrt(HEAD_SIZE)
LEAST_SUM = 1e-25
GREATEST_SUM = 1e30


def attend_kernel(levels, blocks, parts, sources, place_ref, pattern_ref, keep_ref, q_ref, *refs):
    count = len(sources)
    k_refs, v_refs = refs[:count], refs[count : 2 * count]
    out_ref, token_ref = refs[-2:]
    first = place_ref[0] * blocks

    def pick(source, local):
        local = jnp.clip(local, 0, blocks - 1)
        rows = pl.ds(pl.multiple_of(local * BLOCK_TOKENS, BLOCK_TOKENS), BLOCK_TOKENS)
        return k_refs[source][rows, :], v_refs[source][rows, :]

    def gather(block):
        k_part, v_part = pick(0, block)
        ones = jnp.ones_like(v_part)
        k_parts, v_parts, lives = [k_part], [jnp.concatenate([v_part, ones], 1)], []
        for level in range(levels):
            span = 2**level
            named = pattern_ref[first + block, level]
            if span < blocks:
                local = named - first
                near_k, near_v = pick(0, local)
                far_k, far_v = pick(sources.index(1), local + blocks)
                k_part = jnp.where(local >= 0, near_k, far_k)
                v_part = jnp.where(local >= 0, near_v, far_v)
            else:
                shift = span // blocks
                k_part, v_part = pick(sources.index(shift), named - first + shift * blocks)
            live = keep_ref[first + block, level] > 0
            factor = jnp.where(live, 1.0, 0.0).astype(jnp.bfloat16)
            k_parts.append(k_part * factor)
            v_parts.append(jnp.concatenate([v_part * factor, ones * factor], 1))
            lives.append(live)
        return jnp.concatenate(k_parts, 0), jnp.concatenate(v_parts, 0), lives

    def query_rows(part, heads):
        rows = slice(part * BLOCK_TOKENS, (part + 1) * BLOCK_TOKENS)
        return jnp.concatenate(
            [q_ref[rows, h * HEAD_SIZE : (h + 1) * HEAD_SIZE] for h in heads], 0
        )

    def score(q, k):
        return lax.dot_general(
            q, k, (((1,), (1,)), ((), ())), preferred_element_type=jnp.float32
        )

    def store(part, heads, sums):
        result = (sums[:, :HEAD_SIZE] / sums[:, HEAD_SIZE:]).astype(jnp.bfloat16)
        rows = slice(part * BLOCK_TOKENS, (part + 1) * BLOCK_TOKENS)
        for at, h in enumerate(heads):
            out_ref[rows, h * HEAD_SIZE : (h + 1) * HEAD_SIZE] = result[
                at * BLOCK_TOKENS : (at + 1) * BLOCK_TOKENS
            ]

    def causal_of(heads):
        shape = (heads * BLOCK_TOKENS, BLOCK_TOKENS)
        token = lax.broadcasted_iota(jnp.int32, shape, 0) % BLOCK_TOKENS
        return token >= lax.broadcasted_iota(jnp.int32, shape, 1)

    keys = (levels + 1) * BLOCK_TOKENS
    tiles = [slice(t, min(t + TILE_KEYS, keys)) for t in range(0, keys, TILE_KEYS)]
    here = pl.program_id(1) * parts

    def quick():
        gathered = [gather(here + part) for part in range(parts)]
        steps = [
            (part, range(h, h + ROW_HEADS))
            for part in range(parts)
            for h in range(0, GROUP, ROW_HEADS)
        ]
        causal = causal_of(ROW_HEADS)

        def score_tile(step, tile):
            part, heads = step
            return score(query_rows(part, heads), gathered[part][0][tile])

        def finish(step, weights):
            part, heads = step
            sums = jnp.dot(weights, gathered[part][1], preferred_element_type=jnp.float32)
            total = sums[:, HEAD_SIZE:]
            fine = (total > LEAST_SUM) & (total < GREATEST_SUM)
            store(part, heads, sums)
            return jnp.max(jnp.where(fine, 0.0, 1.0).reshape(-1, 8, HEAD_SIZE), axis=0)

        bad = jnp.zeros((8, HEAD_SIZE), jnp.float32)
        scores = [score_tile(steps[0], tile) for tile in tiles]
        last = None
        for at, step in enumerate(steps):
            ahead, weights = [], []
            for t, tile in enumerate(tiles):
                if at + 1 < len(steps):
                    ahead.append(score_tile(steps[at + 1], tile))
                weight = jnp.exp2(scores[t] * SCALE)
                if t == 0:
                    diag = jnp.where(causal, weight[:, :BLOCK_TOKENS], 0.0)
                    weight = jnp.concatenate([diag, weight[:, BLOCK_TOKENS:]], 1)
                weights.append(weight.astype(jnp.bfloat16))
                if t == 0 and last is not None:
                    bad = jnp.maximum(bad, finish(*last))
            last = step, jnp.concatenate(weights, 1)
            scores = ahead
        return jnp.maximum(bad, finish(*last))

    def careful():
        for part in range(parts):
            k, v, lives = gather(here + part)
            bias = jnp.concatenate(
                [
                    jnp.full((1, BLOCK_TOKENS), jnp.where(live, 0.0, MASKED), jnp.float32)
                    for live in lives
                ],
                1,
            )
            causal = causal_of(1)
            for h in range(GROUP):
                scores = score(query_rows(part, [h]), k)
                diag = jnp.where(causal, scores[:, :BLOCK_TOKENS], MASKED)
                scores = jnp.concatenate([diag, scores[:, BLOCK_TOKENS:] + bias], 1)
                peak = jnp.max(scores, axis=1, keepdims=True)
                weights = jnp.exp2((scores - peak) * SCALE).astype(jnp.bfloat16)
                store(part, [h], jnp.dot(weights, v, preferred_element_type=jnp.float32))

    token_ref[0] = 0
    bad = jnp.max(quick())
    pl.when(bad > 0.0)(careful)


def attend_chunk(queries, held, sources, place, pattern, keep, first_head, heads, total, out):
    rows, width = queries.shape
    blocks = rows // BLOCK_TOKENS
    levels = (blocks * total - 1).bit_length()
    group_width = GROUP * HEAD_SIZE

    parts = math.gcd(blocks, STEP_BLOCKS)
    q_block = (parts * BLOCK_TOKENS, group_width)

    def q_index(head, step, *_):
        return step, first_head + head

    in_specs = [pl.BlockSpec(q_block, q_index)]
    operands = [queries]
    for offset in (0, heads):
        for source in sources:
            in_specs.append(
                pl.BlockSpec((rows, HEAD_SIZE), lambda head, step, *_, o=offset: (0, o + head))
            )
            operands.append(held[source])
    aliases = {}
    if out is not None:
        in_specs.append(pl.BlockSpec(memory_space=pl.ANY))
        aliases = {3 + len(operands): 0}
        operands.append(out)
    return pl.pallas_call(
        functools.partial(attend_kernel, levels, blocks, parts, sources),
        grid_spec=pltpu.PrefetchScalarGridSpec(
            num_scalar_prefetch=3,
            grid=(heads, blocks // parts),
            in_specs=in_specs,
            out_specs=[
                pl.BlockSpec(q_block, q_index),
                pl.BlockSpec(memory_space=pltpu.SMEM),
            ],
        ),
        out_shape=[
            jax.ShapeDtypeStruct((rows, width), jnp.bfloat16),
            jax.ShapeDtypeStruct((1,), jnp.int32),
        ],
        input_output_aliases=aliases,
        compiler_params=pltpu.CompilerParams(vmem_limit_bytes=44 * 2**20),
        cost_estimate=pl.CostEstimate(
            flops=1,
            bytes_accessed=1,
            transcendentals=1,
        ),
    )(place, pattern, keep, *operands)


def zero_after(*others):
    total = jnp.int32(0)
    for other in others:
        if jnp.issubdtype(other.dtype, jnp.integer):
            total += other.reshape(-1)[0]
        else:
            corner = other[0, 0].astype(jnp.float32)
            total += (corner != corner).astype(jnp.int32)
    return total


def body(queries, keys, values, pattern, keep):
    total = lax.axis_size(AXES)
    place = lax.axis_index(AXES).astype(jnp.int32)
    sources = tuple([0] + [2**b for b in range(total.bit_length() - 1)])
    stride = max(total // 4, 1)
    up = [(p, p + stride) for p in range(total - stride)]
    up_far = [(s, t) for s, t in up if s >= stride]
    chunks = range(len(CHUNKS))
    firsts = [sum(CHUNKS[:c]) for c in chunks]
    held = []
    for first, heads in zip(firsts, CHUNKS):
        columns = slice(first * HEAD_SIZE, (first + heads) * HEAD_SIZE)
        kv = jnp.concatenate([keys[:, columns], values[:, columns]], 1)
        held.append({0: lax.optimization_barrier(kv)})

    def climb(chunk):
        held[chunk][stride] = lax.ppermute(held[chunk][0], AXES, up)

    def climb_again(chunk):
        held[chunk][2 * stride] = lax.ppermute(held[chunk][stride], AXES, up_far)

    def swap(chunk, distance, *others):
        mine = held[chunk]
        upper = (place & distance) > zero_after(*others)
        sent = jnp.where(upper, mine[2 * distance], mine[0])
        mine[distance] = lax.ppermute(sent, AXES, [(p, p ^ distance) for p in range(total)])

    state = [None, None]

    def attend(chunk):
        state[:] = attend_chunk(
            queries,
            held[chunk],
            sources,
            place.reshape(1),
            pattern,
            keep,
            firsts[chunk],
            CHUNKS[chunk],
            total,
            state[0],
        )

    for chunk in chunks:
        climb(chunk)
    for chunk in chunks:
        climb_again(chunk)
    distances = [stride >> k for k in range(1, stride.bit_length())]
    for chunk in chunks[:-1]:
        for distance in distances:
            early = chunk == chunks[-2] and distance == distances[1]
            swap(chunk, distance, *([]))
    attend(0)
    for distance in distances:
        others = []
        if distance == distances[1]:
            others = [state[1]]
        if distance == distances[-1]:
            attend(1)
            others = [state[1]]
        swap(chunks[-1], distance, *others)
    attend(2)
    attend(3)
    return state[0]


def solution(mesh):
    return jax.shard_map(
        body,
        mesh=mesh,
        in_specs=(P(AXES, None), P(AXES, None), P(AXES, None), P(), P()),
        out_specs=P(AXES, None),
        check_vma=False,
    )
```

```python
import functools
import math

import jax
import jax.numpy as jnp
from jax import lax
from jax.experimental import pallas as pl
from jax.experimental.pallas import tpu as pltpu
from jax.sharding import PartitionSpec as P

QUERY_HEADS = 64
KEY_VALUE_HEADS = 8
HEAD_SIZE = 128
BLOCK_TOKENS = 128
GROUP = QUERY_HEADS // KEY_VALUE_HEADS
AXES = ("seq", "head")
CHUNKS = (2, 2, 2, 2)
ROW_HEADS = 4
TILE_KEYS = 256
STEP_BLOCKS = 2
MASKED = -1e30
SCALE = math.log2(math.e) / math.sqrt(HEAD_SIZE)
LN2 = math.log(2.0)
LEAST_SUM = 1e-25
GREATEST_SUM = 1e30


def power(x):
    near = x.astype(jnp.bfloat16)
    rest = (x - near.astype(jnp.float32)).astype(jnp.bfloat16) * LN2
    return jnp.exp2(near) * (1.0 + rest * (1.0 + 0.5 * rest)).astype(jnp.bfloat16)


def attend_kernel(levels, blocks, parts, sources, place_ref, pattern_ref, keep_ref, q_ref, *refs):
    count = len(sources)
    k_refs, v_refs = refs[:count], refs[count : 2 * count]
    out_ref, token_ref = refs[-2:]
    first = place_ref[0] * blocks

    def pick(source, local):
        local = jnp.clip(local, 0, blocks - 1)
        rows = pl.ds(pl.multiple_of(local * BLOCK_TOKENS, BLOCK_TOKENS), BLOCK_TOKENS)
        return k_refs[source][rows, :], v_refs[source][rows, :]

    def gather(block):
        k_part, v_part = pick(0, block)
        ones = jnp.ones_like(v_part)
        k_parts, v_parts, lives = [k_part], [jnp.concatenate([v_part, ones], 1)], []
        for level in range(levels):
            span = 2**level
            named = pattern_ref[first + block, level]
            if span < blocks:
                local = named - first
                near_k, near_v = pick(0, local)
                far_k, far_v = pick(sources.index(1), local + blocks)
                k_part = jnp.where(local >= 0, near_k, far_k)
                v_part = jnp.where(local >= 0, near_v, far_v)
            else:
                shift = span // blocks
                k_part, v_part = pick(sources.index(shift), named - first + shift * blocks)
            live = keep_ref[first + block, level] > 0
            factor = jnp.where(live, 1.0, 0.0).astype(jnp.bfloat16)
            k_parts.append(k_part * factor)
            v_parts.append(jnp.concatenate([v_part * factor, ones * factor], 1))
            lives.append(live)
        return jnp.concatenate(k_parts, 0), jnp.concatenate(v_parts, 0), lives

    def query_rows(part, heads):
        rows = slice(part * BLOCK_TOKENS, (part + 1) * BLOCK_TOKENS)
        return jnp.concatenate(
            [q_ref[rows, h * HEAD_SIZE : (h + 1) * HEAD_SIZE] for h in heads], 0
        )

    def score(q, k):
        return lax.dot_general(
            q, k, (((1,), (1,)), ((), ())), preferred_element_type=jnp.float32
        )

    def store(part, heads, sums):
        result = (sums[:, :HEAD_SIZE] / sums[:, HEAD_SIZE:]).astype(jnp.bfloat16)
        rows = slice(part * BLOCK_TOKENS, (part + 1) * BLOCK_TOKENS)
        for at, h in enumerate(heads):
            out_ref[rows, h * HEAD_SIZE : (h + 1) * HEAD_SIZE] = result[
                at * BLOCK_TOKENS : (at + 1) * BLOCK_TOKENS
            ]

    def causal_of(heads):
        shape = (heads * BLOCK_TOKENS, BLOCK_TOKENS)
        token = lax.broadcasted_iota(jnp.int32, shape, 0) % BLOCK_TOKENS
        return token >= lax.broadcasted_iota(jnp.int32, shape, 1)

    keys = (levels + 1) * BLOCK_TOKENS
    tiles = [slice(t, min(t + TILE_KEYS, keys)) for t in range(0, keys, TILE_KEYS)]
    here = pl.program_id(1) * parts

    def quick():
        gathered = [gather(here + part) for part in range(parts)]
        steps = [
            (part, range(h, h + ROW_HEADS))
            for part in range(parts)
            for h in range(0, GROUP, ROW_HEADS)
        ]
        causal = causal_of(ROW_HEADS)

        def score_tile(step, tile):
            part, heads = step
            return score(query_rows(part, heads), gathered[part][0][tile])

        def finish(step, weights):
            part, heads = step
            sums = jnp.dot(weights, gathered[part][1], preferred_element_type=jnp.float32)
            total = sums[:, HEAD_SIZE:]
            fine = (total > LEAST_SUM) & (total < GREATEST_SUM)
            store(part, heads, sums)
            return jnp.max(jnp.where(fine, 0.0, 1.0).reshape(-1, 8, HEAD_SIZE), axis=0)

        bad = jnp.zeros((8, HEAD_SIZE), jnp.float32)
        scores = [score_tile(steps[0], tile) for tile in tiles]
        last = None
        for at, step in enumerate(steps):
            ahead, weights = [], []
            for t, tile in enumerate(tiles):
                if at + 1 < len(steps):
                    ahead.append(score_tile(steps[at + 1], tile))
                weight = power(scores[t] * SCALE)
                if t == 0:
                    diag = jnp.where(causal, weight[:, :BLOCK_TOKENS], 0.0).astype(jnp.bfloat16)
                    weight = jnp.concatenate([diag, weight[:, BLOCK_TOKENS:]], 1)
                weights.append(weight)
                if t == 0 and last is not None:
                    bad = jnp.maximum(bad, finish(*last))
            last = step, jnp.concatenate(weights, 1)
            scores = ahead
        return jnp.maximum(bad, finish(*last))

    def careful():
        for part in range(parts):
            k, v, lives = gather(here + part)
            bias = jnp.concatenate(
                [
                    jnp.full((1, BLOCK_TOKENS), jnp.where(live, 0.0, MASKED), jnp.float32)
                    for live in lives
                ],
                1,
            )
            causal = causal_of(1)
            for h in range(GROUP):
                scores = score(query_rows(part, [h]), k)
                diag = jnp.where(causal, scores[:, :BLOCK_TOKENS], MASKED)
                scores = jnp.concatenate([diag, scores[:, BLOCK_TOKENS:] + bias], 1)
                peak = jnp.max(scores, axis=1, keepdims=True)
                weights = jnp.exp2((scores - peak) * SCALE).astype(jnp.bfloat16)
                store(part, [h], jnp.dot(weights, v, preferred_element_type=jnp.float32))

    token_ref[0] = 0
    bad = jnp.max(quick())
    pl.when(bad > 0.0)(careful)


def attend_chunk(queries, held, sources, place, pattern, keep, first_head, heads, total, out):
    rows, width = queries.shape
    blocks = rows // BLOCK_TOKENS
    levels = (blocks * total - 1).bit_length()
    group_width = GROUP * HEAD_SIZE

    parts = math.gcd(blocks, STEP_BLOCKS)
    q_block = (parts * BLOCK_TOKENS, group_width)

    def q_index(head, step, *_):
        return step, first_head + head

    in_specs = [pl.BlockSpec(q_block, q_index)]
    operands = [queries]
    for offset in (0, heads):
        for source in sources:
            in_specs.append(
                pl.BlockSpec((rows, HEAD_SIZE), lambda head, step, *_, o=offset: (0, o + head))
            )
            operands.append(held[source])
    aliases = {}
    if out is not None:
        in_specs.append(pl.BlockSpec(memory_space=pl.ANY))
        aliases = {3 + len(operands): 0}
        operands.append(out)
    return pl.pallas_call(
        functools.partial(attend_kernel, levels, blocks, parts, sources),
        grid_spec=pltpu.PrefetchScalarGridSpec(
            num_scalar_prefetch=3,
            grid=(heads, blocks // parts),
            in_specs=in_specs,
            out_specs=[
                pl.BlockSpec(q_block, q_index),
                pl.BlockSpec(memory_space=pltpu.SMEM),
            ],
        ),
        out_shape=[
            jax.ShapeDtypeStruct((rows, width), jnp.bfloat16),
            jax.ShapeDtypeStruct((1,), jnp.int32),
        ],
        input_output_aliases=aliases,
        compiler_params=pltpu.CompilerParams(vmem_limit_bytes=44 * 2**20),
        cost_estimate=pl.CostEstimate(
            flops=1,
            bytes_accessed=1,
            transcendentals=1,
        ),
    )(place, pattern, keep, *operands)


def zero_after(*others):
    total = jnp.int32(0)
    for other in others:
        if jnp.issubdtype(other.dtype, jnp.integer):
            total += other.reshape(-1)[0]
        else:
            corner = other[0, 0].astype(jnp.float32)
            total += (corner != corner).astype(jnp.int32)
    return total


def body(queries, keys, values, pattern, keep):
    total = lax.axis_size(AXES)
    place = lax.axis_index(AXES).astype(jnp.int32)
    sources = tuple([0] + [2**b for b in range(total.bit_length() - 1)])
    stride = max(total // 4, 1)
    up = [(p, p + stride) for p in range(total - stride)]
    up_far = [(s, t) for s, t in up if s >= stride]
    chunks = range(len(CHUNKS))
    firsts = [sum(CHUNKS[:c]) for c in chunks]
    held = []
    for first, heads in zip(firsts, CHUNKS):
        columns = slice(first * HEAD_SIZE, (first + heads) * HEAD_SIZE)
        kv = jnp.concatenate([keys[:, columns], values[:, columns]], 1)
        held.append({0: lax.optimization_barrier(kv)})

    def climb(chunk):
        held[chunk][stride] = lax.ppermute(held[chunk][0], AXES, up)

    def climb_again(chunk):
        held[chunk][2 * stride] = lax.ppermute(held[chunk][stride], AXES, up_far)

    def swap(chunk, distance, *others):
        mine = held[chunk]
        upper = (place & distance) > zero_after(*others)
        sent = jnp.where(upper, mine[2 * distance], mine[0])
        mine[distance] = lax.ppermute(sent, AXES, [(p, p ^ distance) for p in range(total)])

    state = [None, None]

    def attend(chunk):
        state[:] = attend_chunk(
            queries,
            held[chunk],
            sources,
            place.reshape(1),
            pattern,
            keep,
            firsts[chunk],
            CHUNKS[chunk],
            total,
            state[0],
        )

    for chunk in chunks:
        climb(chunk)
    for chunk in chunks:
        climb_again(chunk)
    distances = [stride >> k for k in range(1, stride.bit_length())]
    for chunk in chunks[:-1]:
        for distance in distances:
            early = chunk == chunks[-2] and distance == distances[1]
            swap(chunk, distance, *([]))
    attend(0)
    for distance in distances:
        others = []
        if distance == distances[1]:
            others = [state[1]]
        if distance == distances[-1]:
            attend(1)
            others = [state[1]]
        swap(chunks[-1], distance, *others)
    attend(2)
    attend(3)
    return state[0]


def solution(mesh):
    return jax.shard_map(
        body,
        mesh=mesh,
        in_specs=(P(AXES, None), P(AXES, None), P(AXES, None), P(), P()),
        out_specs=P(AXES, None),
        check_vma=False,
    )
```

```python
import functools
import math

import jax
import jax.numpy as jnp
from jax import lax
from jax.experimental import pallas as pl
from jax.experimental.pallas import tpu as pltpu
from jax.sharding import PartitionSpec as P

QUERY_HEADS = 64
KEY_VALUE_HEADS = 8
HEAD_SIZE = 128
BLOCK_TOKENS = 128
GROUP = QUERY_HEADS // KEY_VALUE_HEADS
AXES = ("seq", "head")
CHUNKS = (2, 2, 2, 2)
ROW_HEADS = 4
TILE_KEYS = 256
STEP_BLOCKS = 2
MASKED = -1e30
SCALE = math.log2(math.e) / math.sqrt(HEAD_SIZE)
LEAST_SUM = 1e-25
GREATEST_SUM = 1e30


def slots_of(levels, blocks, block, mode):
    own = [None] + [level for level in range(levels) if 2**level <= block]
    rest = [level for level in range(levels) if level not in own]
    return {"own": own, "rest": rest, "all": own + rest}[mode]


def attend_kernel(levels, blocks, parts, sources, mode, place_ref, pattern_ref, keep_ref, q_ref, *refs):
    count = len(sources)
    k_refs, v_refs = refs[:count], refs[count : 2 * count]
    kt_ref = refs[-1]
    token_ref = refs[-2]
    out_ref = refs[-3]
    sums_ref = refs[2 * count] if mode == "rest" else refs[-3]
    first = place_ref[0] * blocks

    def pick(source, local):
        local = jnp.clip(local, 0, blocks - 1)
        rows = pl.ds(pl.multiple_of(local * BLOCK_TOKENS, BLOCK_TOKENS), BLOCK_TOKENS)
        return kt_ref[source, :, rows], v_refs[source][rows, :]

    def gather(block, slots):
        k_parts, v_parts, lives = [], [], []
        ones = jnp.ones((BLOCK_TOKENS, HEAD_SIZE), jnp.bfloat16)
        for slot in slots:
            if slot is None:
                k_part, v_part = pick(0, block)
                k_parts.append(k_part)
                v_parts.append(jnp.concatenate([v_part, ones], 1))
                continue
            span = 2**slot
            shift = 0 if span <= block else max(span // blocks, 1)
            named = pattern_ref[first + block, slot]
            k_part, v_part = pick(sources.index(shift), named - first + shift * blocks)
            live = keep_ref[first + block, slot] > 0
            factor = jnp.where(live, 1.0, 0.0).astype(jnp.bfloat16)
            k_parts.append(k_part * factor)
            v_parts.append(jnp.concatenate([v_part * factor, ones * factor], 1))
            lives.append(live)
        return jnp.concatenate(k_parts, 1), jnp.concatenate(v_parts, 0), lives

    def rows_of(part):
        return slice(part * BLOCK_TOKENS, (part + 1) * BLOCK_TOKENS)

    def query_rows(part, heads):
        return jnp.concatenate(
            [q_ref[rows_of(part), h * HEAD_SIZE : (h + 1) * HEAD_SIZE] for h in heads], 0
        )

    def score(q, k):
        return jnp.dot(q, k, preferred_element_type=jnp.float32)

    def store(part, heads, sums):
        total = sums[:, HEAD_SIZE:]
        inverse = pl.reciprocal(total, approx=True)
        inverse = inverse * (2.0 - total * inverse)
        result = (sums[:, :HEAD_SIZE] * inverse).astype(jnp.bfloat16)
        for at, h in enumerate(heads):
            out_ref[rows_of(part), h * HEAD_SIZE : (h + 1) * HEAD_SIZE] = result[rows_of(at)]

    def causal_of(heads):
        shape = (heads * BLOCK_TOKENS, BLOCK_TOKENS)
        token = lax.broadcasted_iota(jnp.int32, shape, 0) % BLOCK_TOKENS
        return token >= lax.broadcasted_iota(jnp.int32, shape, 1)

    def quick(here):
        slots = [slots_of(levels, blocks, here + part, mode) for part in range(parts)]
        gathered = [gather(here + part, slots[part]) for part in range(parts)]
        steps = [
            (part, range(h, h + ROW_HEADS))
            for part in range(parts)
            for h in range(0, GROUP, ROW_HEADS)
        ]
        causal = causal_of(ROW_HEADS)

        def score_tiles(step):
            part, heads = step
            keys = len(slots[part]) * BLOCK_TOKENS
            tiles = [slice(t, min(t + TILE_KEYS, keys)) for t in range(0, keys, TILE_KEYS)]
            return [lambda t=t: score(query_rows(part, heads), gathered[part][0][:, t]) for t in tiles]

        def finish(step, weights):
            part, heads = step
            sums = jnp.dot(weights, gathered[part][1], preferred_element_type=jnp.float32)
            width = 2 * HEAD_SIZE
            if mode == "own":
                for at, h in enumerate(heads):
                    sums_ref[rows_of(part), h * width : (h + 1) * width] = sums[rows_of(at)]
                return None
            sums += jnp.concatenate(
                [sums_ref[rows_of(part), h * width : (h + 1) * width] for h in heads], 0
            )
            store(part, heads, sums)
            total = sums[:, HEAD_SIZE:].reshape(-1, 8, HEAD_SIZE)
            return jnp.min(total, axis=0), jnp.max(total, axis=0)

        seen = []
        scores = [tile() for tile in score_tiles(steps[0])]
        last = None
        for at, step in enumerate(steps):
            todo = score_tiles(steps[at + 1]) if at + 1 < len(steps) else []
            ahead, weights = [], []
            for t, tile_scores in enumerate(scores):
                if t < len(todo):
                    ahead.append(todo[t]())
                weight = jnp.exp2(tile_scores * SCALE)
                if t == 0 and slots[step[0]][0] is None:
                    diag = jnp.where(causal, weight[:, :BLOCK_TOKENS], 0.0)
                    rest = weight[:, BLOCK_TOKENS:] if weight.shape[1] > BLOCK_TOKENS else None
                    weight = diag if rest is None else jnp.concatenate([diag, rest], 1)
                weights.append(weight.astype(jnp.bfloat16))
                if t == 0 and last is not None:
                    seen.append(finish(*last))
            ahead += [tile() for tile in todo[len(scores) :]]
            last = step, jnp.concatenate(weights, 1)
            scores = ahead
        seen.append(finish(*last))
        if mode == "own":
            return
        least = functools.reduce(jnp.minimum, [low for low, _ in seen])
        greatest = functools.reduce(jnp.maximum, [high for _, high in seen])
        fine = (jnp.min(least) > LEAST_SUM) & (jnp.max(greatest) < GREATEST_SUM)
        pl.when(jnp.logical_not(fine))(lambda: careful(here))

    def careful(here):
        causal = causal_of(1)
        for part in range(parts):
            k, v, lives = gather(here + part, slots_of(levels, blocks, here + part, "all"))
            bias = jnp.concatenate(
                [
                    jnp.full((1, BLOCK_TOKENS), jnp.where(live, 0.0, MASKED), jnp.float32)
                    for live in lives
                ],
                1,
            )
            for h in range(GROUP):
                scores = score(query_rows(part, [h]), k)
                diag = jnp.where(causal, scores[:, :BLOCK_TOKENS], MASKED)
                scores = jnp.concatenate([diag, scores[:, BLOCK_TOKENS:] + bias], 1)
                peak = jnp.max(scores, axis=1, keepdims=True)
                weights = jnp.exp2((scores - peak) * SCALE).astype(jnp.bfloat16)
                store(part, [h], jnp.dot(weights, v, preferred_element_type=jnp.float32))

    token_ref[0] = 0

    @pl.when(pl.program_id(1) == 0)
    def _():
        for source in range(count):
            kt_ref[source] = k_refs[source][...].T

    for step in range(blocks // parts):
        pl.when(pl.program_id(1) == step)(functools.partial(quick, step * parts))


def attend_chunk(mode, queries, held, sources, place, pattern, keep, first_head, heads, total, sums, out):
    rows, width = queries.shape
    blocks = rows // BLOCK_TOKENS
    levels = (blocks * total - 1).bit_length()
    group_width = GROUP * HEAD_SIZE
    parts = math.gcd(blocks, STEP_BLOCKS)
    q_block = (parts * BLOCK_TOKENS, group_width)
    sums_spec = pl.BlockSpec((parts * BLOCK_TOKENS, 2 * group_width), lambda head, step, *_: (step, head))

    def q_index(head, step, *_):
        return step, first_head + head

    in_specs = [pl.BlockSpec(q_block, q_index)]
    operands = [queries]
    for offset in (0, heads):
        for source in sources:
            in_specs.append(
                pl.BlockSpec((rows, HEAD_SIZE), lambda head, step, *_, o=offset: (0, o + head))
            )
            operands.append(held[source])
    aliases = {}
    if mode == "own":
        out_spec = sums_spec
        out_shape = jax.ShapeDtypeStruct((rows, 2 * group_width * heads), jnp.float32)
    else:
        out_spec = pl.BlockSpec(q_block, q_index)
        out_shape = jax.ShapeDtypeStruct((rows, width), jnp.bfloat16)
        in_specs.append(sums_spec)
        operands.append(sums)
        if out is not None:
            in_specs.append(pl.BlockSpec(memory_space=pl.ANY))
            aliases = {3 + len(operands): 0}
            operands.append(out)
    return pl.pallas_call(
        functools.partial(attend_kernel, levels, blocks, parts, sources, mode),
        grid_spec=pltpu.PrefetchScalarGridSpec(
            num_scalar_prefetch=3,
            grid=(heads, blocks // parts),
            in_specs=in_specs,
            out_specs=[out_spec, pl.BlockSpec(memory_space=pltpu.SMEM)],
            scratch_shapes=[pltpu.VMEM((len(sources), HEAD_SIZE, rows), jnp.bfloat16)],
        ),
        out_shape=[out_shape, jax.ShapeDtypeStruct((1,), jnp.int32)],
        input_output_aliases=aliases,
        compiler_params=pltpu.CompilerParams(vmem_limit_bytes=44 * 2**20),
        cost_estimate=pl.CostEstimate(flops=1, bytes_accessed=1, transcendentals=1),
    )(place, pattern, keep, *operands)


def zero_after(*others):
    total = jnp.int32(0)
    for other in others:
        if jnp.issubdtype(other.dtype, jnp.integer):
            total += other.reshape(-1)[0]
        else:
            corner = other[0, 0].astype(jnp.float32)
            total += (corner != corner).astype(jnp.int32)
    return total


def body(queries, keys, values, pattern, keep):
    total = lax.axis_size(AXES)
    place = lax.axis_index(AXES).astype(jnp.int32)
    sources = tuple([0] + [2**b for b in range(total.bit_length() - 1)])
    stride = max(total // 4, 1)
    up = [(p, p + stride) for p in range(total - stride)]
    up_far = [(s, t) for s, t in up if s >= stride]
    chunks = range(len(CHUNKS))
    firsts = [sum(CHUNKS[:c]) for c in chunks]
    held = []

    def climb(chunk):
        columns = slice(firsts[chunk] * HEAD_SIZE, (firsts[chunk] + CHUNKS[chunk]) * HEAD_SIZE)
        kv = jnp.concatenate([keys[:, columns], values[:, columns]], 1)
        kv = lax.optimization_barrier(kv)
        held.append({0: kv, stride: lax.ppermute(kv, AXES, up)})

    def climb_again(chunk):
        held[chunk][2 * stride] = lax.ppermute(held[chunk][stride], AXES, up_far)

    def swap(chunk, distance, *others):
        mine = held[chunk]
        upper = (place & distance) > zero_after(*others)
        sent = jnp.where(upper, mine[2 * distance], mine[0])
        mine[distance] = lax.ppermute(sent, AXES, [(p, p ^ distance) for p in range(total)])

    own = {}
    state = [None, None]

    def common(chunk):
        return place.reshape(1), pattern, keep, firsts[chunk], CHUNKS[chunk], total

    def attend_own(chunk):
        own[chunk] = attend_chunk(
            "own", queries, held[chunk], (0,), *common(chunk), None, None
        )

    def attend(chunk):
        state[:] = attend_chunk(
            "rest", queries, held[chunk], sources, *common(chunk), own[chunk][0], state[0]
        )

    for chunk in chunks:
        climb(chunk)
        attend_own(chunk)
    for chunk in chunks:
        climb_again(chunk)
    distances = [stride >> k for k in range(1, stride.bit_length())]
    near, nearest = distances[1], distances[-1]
    waits = {
        (1, distances[0]): lambda: [own[0][1], own[1][1]],
        (2, distances[0]): lambda: [own[2][1]],
        (3, distances[0]): lambda: [own[3][1]],
        (3, near): lambda: [tokens[0]],
        (3, nearest): lambda: [tokens[1]],
    }
    tokens = {}
    for chunk in chunks:
        for distance in distances:
            if (chunk, distance) == (3, nearest):
                attend(1)
                tokens[1] = state[1]
            swap(chunk, distance, *waits.get((chunk, distance), list)())
        if chunk == 0:
            attend(0)
            tokens[0] = state[1]
    attend(2)
    attend(3)
    return state[0]


def solution(mesh):
    return jax.shard_map(
        body,
        mesh=mesh,
        in_specs=(P(AXES, None), P(AXES, None), P(AXES, None), P(), P()),
        out_specs=P(AXES, None),
        check_vma=False,
    )
```

```python
import functools
import math

import jax
import jax.numpy as jnp
from jax import lax
from jax.experimental import pallas as pl
from jax.experimental.pallas import tpu as pltpu
from jax.sharding import PartitionSpec as P

QUERY_HEADS = 64
KEY_VALUE_HEADS = 8
HEAD_SIZE = 128
BLOCK_TOKENS = 128
GROUP = QUERY_HEADS // KEY_VALUE_HEADS
AXES = ("seq", "head")
CHUNKS = (2, 2, 2, 2)
ROW_HEADS = 2
STEP_BLOCKS = 2
MASKED = -1e30
SCALE = math.log2(math.e) / math.sqrt(HEAD_SIZE)
LEAST_SUM = 1e-25
GREATEST_SUM = 1e30


def attend_kernel(levels, blocks, parts, sources, place_ref, pattern_ref, keep_ref, q_ref, *refs):
    count = len(sources)
    k_refs, v_refs = refs[:count], refs[count : 2 * count]
    out_ref, token_ref = refs[-2:]
    first = place_ref[0] * blocks

    def pick(source, local):
        local = jnp.clip(local, 0, blocks - 1)
        rows = pl.ds(pl.multiple_of(local * BLOCK_TOKENS, BLOCK_TOKENS), BLOCK_TOKENS)
        return k_refs[source][rows, :], v_refs[source][rows, :]

    def gather(block):
        k_part, v_part = pick(0, block)
        ones = jnp.ones_like(v_part)
        k_parts, v_parts, lives = [k_part], [jnp.concatenate([v_part, ones], 1)], []
        for level in range(levels):
            span = 2**level
            named = pattern_ref[first + block, level]
            if span < blocks:
                local = named - first
                near_k, near_v = pick(0, local)
                far_k, far_v = pick(sources.index(1), local + blocks)
                k_part = jnp.where(local >= 0, near_k, far_k)
                v_part = jnp.where(local >= 0, near_v, far_v)
            else:
                shift = span // blocks
                k_part, v_part = pick(sources.index(shift), named - first + shift * blocks)
            live = keep_ref[first + block, level] > 0
            factor = jnp.where(live, 1.0, 0.0).astype(jnp.bfloat16)
            k_parts.append(k_part * factor)
            v_parts.append(jnp.concatenate([v_part * factor, ones * factor], 1))
            lives.append(live)
        return jnp.concatenate(k_parts, 0), jnp.concatenate(v_parts, 0), lives

    def query_rows(part, heads):
        rows = slice(part * BLOCK_TOKENS, (part + 1) * BLOCK_TOKENS)
        return jnp.concatenate(
            [q_ref[rows, h * HEAD_SIZE : (h + 1) * HEAD_SIZE] for h in heads], 0
        )

    def score(q, k):
        return lax.dot_general(
            q, k, (((1,), (1,)), ((), ())), preferred_element_type=jnp.float32
        )

    def store(part, heads, sums):
        total = sums[:, HEAD_SIZE:]
        inverse = pl.reciprocal(total, approx=True)
        inverse = inverse * (2.0 - total * inverse)
        result = (sums[:, :HEAD_SIZE] * inverse).astype(jnp.bfloat16)
        rows = slice(part * BLOCK_TOKENS, (part + 1) * BLOCK_TOKENS)
        for at, h in enumerate(heads):
            out_ref[rows, h * HEAD_SIZE : (h + 1) * HEAD_SIZE] = result[
                at * BLOCK_TOKENS : (at + 1) * BLOCK_TOKENS
            ]

    def causal_of(heads):
        shape = (heads * BLOCK_TOKENS, BLOCK_TOKENS)
        token = lax.broadcasted_iota(jnp.int32, shape, 0) % BLOCK_TOKENS
        return token >= lax.broadcasted_iota(jnp.int32, shape, 1)

    here = pl.program_id(1) * parts

    def quick():
        gathered = [gather(here + part) for part in range(parts)]
        steps = [
            (part, range(h, h + ROW_HEADS))
            for part in range(parts)
            for h in range(0, GROUP, ROW_HEADS)
        ]
        causal = causal_of(ROW_HEADS)

        def scores_of(step):
            part, heads = step
            return score(query_rows(part, heads), gathered[part][0])

        least = jnp.full((8, HEAD_SIZE), GREATEST_SUM, jnp.float32)
        greatest = jnp.full((8, HEAD_SIZE), LEAST_SUM, jnp.float32)
        ahead = scores_of(steps[0])
        for at, (part, heads) in enumerate(steps):
            scores = ahead
            if at + 1 < len(steps):
                ahead = scores_of(steps[at + 1])
            weights = jnp.exp2(scores * SCALE)
            diag = jnp.where(causal, weights[:, :BLOCK_TOKENS], 0.0)
            weights = jnp.concatenate([diag, weights[:, BLOCK_TOKENS:]], 1).astype(jnp.bfloat16)
            sums = jnp.dot(weights, gathered[part][1], preferred_element_type=jnp.float32)
            store(part, heads, sums)
            total = sums[:, HEAD_SIZE:].reshape(-1, 8, HEAD_SIZE)
            least = jnp.minimum(least, jnp.min(total, axis=0))
            greatest = jnp.maximum(greatest, jnp.max(total, axis=0))
        return least, greatest

    def careful():
        for part in range(parts):
            k, v, lives = gather(here + part)
            bias = jnp.concatenate(
                [
                    jnp.full((1, BLOCK_TOKENS), jnp.where(live, 0.0, MASKED), jnp.float32)
                    for live in lives
                ],
                1,
            )
            causal = causal_of(1)
            for h in range(GROUP):
                scores = score(query_rows(part, [h]), k)
                diag = jnp.where(causal, scores[:, :BLOCK_TOKENS], MASKED)
                scores = jnp.concatenate([diag, scores[:, BLOCK_TOKENS:] + bias], 1)
                peak = jnp.max(scores, axis=1, keepdims=True)
                weights = jnp.exp2((scores - peak) * SCALE).astype(jnp.bfloat16)
                store(part, [h], jnp.dot(weights, v, preferred_element_type=jnp.float32))

    token_ref[0] = 0
    least, greatest = quick()
    fine = (jnp.min(least) > LEAST_SUM) & (jnp.max(greatest) < GREATEST_SUM)
    pl.when(jnp.logical_not(fine))(careful)


def attend_chunk(queries, held, sources, place, pattern, keep, first_head, heads, total, out):
    rows, width = queries.shape
    blocks = rows // BLOCK_TOKENS
    levels = (blocks * total - 1).bit_length()
    group_width = GROUP * HEAD_SIZE

    parts = math.gcd(blocks, STEP_BLOCKS)
    q_block = (parts * BLOCK_TOKENS, group_width)

    def q_index(head, step, *_):
        return step, first_head + head

    in_specs = [pl.BlockSpec(q_block, q_index)]
    operands = [queries]
    for offset in (0, heads):
        for source in sources:
            in_specs.append(
                pl.BlockSpec((rows, HEAD_SIZE), lambda head, step, *_, o=offset: (0, o + head))
            )
            operands.append(held[source])
    aliases = {}
    if out is not None:
        in_specs.append(pl.BlockSpec(memory_space=pl.ANY))
        aliases = {3 + len(operands): 0}
        operands.append(out)
    return pl.pallas_call(
        functools.partial(attend_kernel, levels, blocks, parts, sources),
        grid_spec=pltpu.PrefetchScalarGridSpec(
            num_scalar_prefetch=3,
            grid=(heads, blocks // parts),
            in_specs=in_specs,
            out_specs=[
                pl.BlockSpec(q_block, q_index),
                pl.BlockSpec(memory_space=pltpu.SMEM),
            ],
        ),
        out_shape=[
            jax.ShapeDtypeStruct((rows, width), jnp.bfloat16),
            jax.ShapeDtypeStruct((1,), jnp.int32),
        ],
        input_output_aliases=aliases,
        compiler_params=pltpu.CompilerParams(vmem_limit_bytes=44 * 2**20),
        cost_estimate=pl.CostEstimate(
            flops=1,
            bytes_accessed=1,
            transcendentals=1,
        ),
    )(place, pattern, keep, *operands)


def zero_after(*others):
    total = jnp.int32(0)
    for other in others:
        if jnp.issubdtype(other.dtype, jnp.integer):
            total += other.reshape(-1)[0]
        else:
            corner = other[0, 0].astype(jnp.float32)
            total += (corner != corner).astype(jnp.int32)
    return total


def body(queries, keys, values, pattern, keep):
    total = lax.axis_size(AXES)
    place = lax.axis_index(AXES).astype(jnp.int32)
    sources = tuple([0] + [2**b for b in range(total.bit_length() - 1)])
    stride = max(total // 4, 1)
    up = [(p, p + stride) for p in range(total - stride)]
    up_far = [(s, t) for s, t in up if s >= stride]
    chunks = range(len(CHUNKS))
    firsts = [sum(CHUNKS[:c]) for c in chunks]
    held = []
    for first, heads in zip(firsts, CHUNKS):
        columns = slice(first * HEAD_SIZE, (first + heads) * HEAD_SIZE)
        kv = jnp.concatenate([keys[:, columns], values[:, columns]], 1)
        held.append({0: lax.optimization_barrier(kv)})

    def climb(chunk):
        held[chunk][stride] = lax.ppermute(held[chunk][0], AXES, up)

    def climb_again(chunk):
        held[chunk][2 * stride] = lax.ppermute(held[chunk][stride], AXES, up_far)

    def swap(chunk, distance, *others):
        mine = held[chunk]
        upper = (place & distance) > zero_after(*others)
        sent = jnp.where(upper, mine[2 * distance], mine[0])
        mine[distance] = lax.ppermute(sent, AXES, [(p, p ^ distance) for p in range(total)])

    state = [None, None]

    def attend(chunk):
        state[:] = attend_chunk(
            queries,
            held[chunk],
            sources,
            place.reshape(1),
            pattern,
            keep,
            firsts[chunk],
            CHUNKS[chunk],
            total,
            state[0],
        )

    distances = [stride >> k for k in range(1, stride.bit_length())]
    middle, near, nearest = distances[0], distances[1], distances[-1]
    for chunk in chunks:
        climb(chunk)
    for chunk in chunks:
        climb_again(chunk)
    tokens = {}
    waits = {
        (2, middle): lambda: [held[0][middle]],
        (3, middle): lambda: [held[0][near], held[1][middle]],
        (2, near): lambda: [held[0][nearest]],
        (3, near): lambda: [held[1][2*stride], tokens[0]],
        (3, nearest): lambda: [tokens[1]],
    }
    for chunk in chunks:
        for distance in distances:
            if (chunk, distance) == (3, nearest):
                attend(1)
                tokens[1] = state[1]
            swap(chunk, distance, *waits.get((chunk, distance), list)())
        if chunk == 0:
            attend(0)
            tokens[0] = state[1]
    attend(2)
    attend(3)
    return state[0]


def solution(mesh):
    return jax.shard_map(
        body,
        mesh=mesh,
        in_specs=(P(AXES, None), P(AXES, None), P(AXES, None), P(), P()),
        out_specs=P(AXES, None),
        check_vma=False,
    )
```

```python
import functools
import math

import jax
import jax.numpy as jnp
from jax import lax
from jax.experimental import pallas as pl
from jax.experimental.pallas import tpu as pltpu
from jax.sharding import PartitionSpec as P

QUERY_HEADS = 64
KEY_VALUE_HEADS = 8
HEAD_SIZE = 128
BLOCK_TOKENS = 128
GROUP = QUERY_HEADS // KEY_VALUE_HEADS
AXES = ("seq", "head")
CHUNKS = (2, 2, 2, 2)
ROW_HEADS = 2
STEP_BLOCKS = 2
MASKED = -1e30
SCALE = math.log2(math.e) / math.sqrt(HEAD_SIZE)
LEAST_SUM = 1e-25
GREATEST_SUM = 1e30


def attend_kernel(levels, blocks, parts, sources, place_ref, pattern_ref, keep_ref, q_ref, *refs):
    count = len(sources)
    k_refs, v_refs = refs[:count], refs[count : 2 * count]
    out_ref, token_ref = refs[-2:]
    first = place_ref[0] * blocks

    def pick(source, local):
        local = jnp.clip(local, 0, blocks - 1)
        rows = pl.ds(pl.multiple_of(local * BLOCK_TOKENS, BLOCK_TOKENS), BLOCK_TOKENS)
        return k_refs[source][rows, :], v_refs[source][rows, :]

    def gather(block):
        k_part, v_part = pick(0, block)
        k_parts, v_parts, lives = [k_part], [v_part], []
        for level in range(levels):
            span = 2**level
            named = pattern_ref[first + block, level]
            if span < blocks:
                local = named - first
                near_k, near_v = pick(0, local)
                far_k, far_v = pick(sources.index(1), local + blocks)
                k_part = jnp.where(local >= 0, near_k, far_k)
                v_part = jnp.where(local >= 0, near_v, far_v)
            else:
                shift = span // blocks
                k_part, v_part = pick(sources.index(shift), named - first + shift * blocks)
            live = keep_ref[first + block, level] > 0
            k_parts.append(k_part)
            v_parts.append(v_part)
            lives.append(live)
        bias = [
            jnp.full((1, BLOCK_TOKENS), jnp.where(live, 0.0, MASKED), jnp.float32) for live in lives
        ]
        return jnp.concatenate(k_parts, 0), jnp.concatenate(v_parts, 0), jnp.concatenate(bias, 1)

    def query_rows(part, heads):
        rows = slice(part * BLOCK_TOKENS, (part + 1) * BLOCK_TOKENS)
        return jnp.concatenate(
            [q_ref[rows, h * HEAD_SIZE : (h + 1) * HEAD_SIZE] for h in heads], 0
        )

    def score(q, k):
        return lax.dot_general(
            q, k, (((1,), (1,)), ((), ())), preferred_element_type=jnp.float32
        )

    def store(part, heads, sums, total):
        result = (sums * (1.0 / total)).astype(jnp.bfloat16)
        rows = slice(part * BLOCK_TOKENS, (part + 1) * BLOCK_TOKENS)
        for at, h in enumerate(heads):
            out_ref[rows, h * HEAD_SIZE : (h + 1) * HEAD_SIZE] = result[
                at * BLOCK_TOKENS : (at + 1) * BLOCK_TOKENS
            ]

    def causal_of(heads):
        shape = (heads * BLOCK_TOKENS, BLOCK_TOKENS)
        token = lax.broadcasted_iota(jnp.int32, shape, 0) % BLOCK_TOKENS
        return token >= lax.broadcasted_iota(jnp.int32, shape, 1)

    here = pl.program_id(1) * parts

    def quick():
        gathered = [gather(here + part) for part in range(parts)]
        steps = [
            (part, range(h, h + ROW_HEADS))
            for part in range(parts)
            for h in range(0, GROUP, ROW_HEADS)
        ]
        causal = causal_of(ROW_HEADS)

        def scores_of(step):
            part, heads = step
            return score(query_rows(part, heads), gathered[part][0])

        least = jnp.full((ROW_HEADS * BLOCK_TOKENS, 1), GREATEST_SUM, jnp.float32)
        greatest = jnp.full((ROW_HEADS * BLOCK_TOKENS, 1), LEAST_SUM, jnp.float32)
        ahead = scores_of(steps[0])
        for at, (part, heads) in enumerate(steps):
            scores = ahead
            if at + 1 < len(steps):
                ahead = scores_of(steps[at + 1])
            diag = jnp.where(causal, scores[:, :BLOCK_TOKENS] * SCALE, MASKED)
            rest = scores[:, BLOCK_TOKENS:] * SCALE + gathered[part][2]
            weights = jnp.exp2(jnp.concatenate([diag, rest], 1))
            total = jnp.sum(weights, axis=1, keepdims=True)
            sums = jnp.dot(
                weights.astype(jnp.bfloat16), gathered[part][1], preferred_element_type=jnp.float32
            )
            store(part, heads, sums, total)
            least = jnp.minimum(least, total)
            greatest = jnp.maximum(greatest, total)
        return least, greatest

    def careful():
        causal = causal_of(1)
        for part in range(parts):
            k, v, bias = gather(here + part)
            for h in range(GROUP):
                scores = score(query_rows(part, [h]), k)
                diag = jnp.where(causal, scores[:, :BLOCK_TOKENS], MASKED)
                scores = jnp.concatenate([diag, scores[:, BLOCK_TOKENS:] + bias], 1)
                peak = jnp.max(scores, axis=1, keepdims=True)
                weights = jnp.exp2((scores - peak) * SCALE)
                total = jnp.sum(weights, axis=1, keepdims=True)
                sums = jnp.dot(weights.astype(jnp.bfloat16), v, preferred_element_type=jnp.float32)
                store(part, [h], sums, total)

    token_ref[0] = 0
    least, greatest = quick()
    fine = (jnp.min(least) > LEAST_SUM) & (jnp.max(greatest) < GREATEST_SUM)
    pl.when(jnp.logical_not(fine))(careful)


def attend_chunk(queries, held, sources, place, pattern, keep, first_head, heads, total, out):
    rows, width = queries.shape
    blocks = rows // BLOCK_TOKENS
    levels = (blocks * total - 1).bit_length()
    group_width = GROUP * HEAD_SIZE

    parts = math.gcd(blocks, STEP_BLOCKS)
    q_block = (parts * BLOCK_TOKENS, group_width)

    def q_index(head, step, *_):
        return step, first_head + head

    in_specs = [pl.BlockSpec(q_block, q_index)]
    operands = [queries]
    for offset in (0, heads):
        for source in sources:
            array, column = held[source]
            in_specs.append(
                pl.BlockSpec(
                    (rows, HEAD_SIZE), lambda head, step, *_, o=column + offset: (0, o + head)
                )
            )
            operands.append(array)
    aliases = {}
    if out is not None:
        in_specs.append(pl.BlockSpec(memory_space=pl.ANY))
        aliases = {3 + len(operands): 0}
        operands.append(out)
    return pl.pallas_call(
        functools.partial(attend_kernel, levels, blocks, parts, sources),
        grid_spec=pltpu.PrefetchScalarGridSpec(
            num_scalar_prefetch=3,
            grid=(heads, blocks // parts),
            in_specs=in_specs,
            out_specs=[
                pl.BlockSpec(q_block, q_index),
                pl.BlockSpec(memory_space=pltpu.SMEM),
            ],
        ),
        out_shape=[
            jax.ShapeDtypeStruct((rows, width), jnp.bfloat16),
            jax.ShapeDtypeStruct((1,), jnp.int32),
        ],
        input_output_aliases=aliases,
        compiler_params=pltpu.CompilerParams(vmem_limit_bytes=44 * 2**20),
        cost_estimate=pl.CostEstimate(
            flops=5000000000,
            bytes_accessed=1,
            transcendentals=1,
        ),
    )(place, pattern, keep, *operands)


def zero_after(*others):
    total = jnp.int32(0)
    for other in others:
        if jnp.issubdtype(other.dtype, jnp.integer):
            total += other.reshape(-1)[0]
        else:
            corner = other[0, 0].astype(jnp.float32)
            total += (corner != corner).astype(jnp.int32)
    return total


def body(queries, keys, values, pattern, keep):
    total = lax.axis_size(AXES)
    place = lax.axis_index(AXES).astype(jnp.int32)
    sources = tuple([0] + [2**b for b in range(total.bit_length() - 1)])
    stride = max(total // 4, 1)
    up = [(p, p + stride) for p in range(total - stride)]
    chunks = range(len(CHUNKS))
    distances = [stride >> k for k in range(1, stride.bit_length())]
    near, nearest = distances[1], distances[-1]
    firsts = [sum(CHUNKS[:c]) for c in chunks]
    held = []
    for first, heads in zip(firsts, CHUNKS):
        columns = slice(first * HEAD_SIZE, (first + heads) * HEAD_SIZE)
        kv = jnp.concatenate([keys[:, columns], values[:, columns]], 1)
        held.append({0: (lax.optimization_barrier(kv), 0)})

    def part_of(chunk, source):
        array, column = held[chunk][source]
        width = 2 * CHUNKS[chunk] * HEAD_SIZE
        return array[:, column * HEAD_SIZE : column * HEAD_SIZE + width]

    def climb(*moves):
        sent = jnp.concatenate([part_of(*move) for move in moves], 1)
        arrived, column = lax.ppermute(sent, AXES, up), 0
        for chunk, source in moves:
            held[chunk][source + stride] = arrived, column
            column += 2 * CHUNKS[chunk]

    def swap(chunk, distance, *others):
        upper = (place & distance) > zero_after(*others)
        sent = jnp.where(upper, part_of(chunk, 2 * distance), part_of(chunk, 0))
        pairs = [(p, p ^ distance) for p in range(total)]
        held[chunk][distance] = lax.ppermute(sent, AXES, pairs), 0

    state = [None, None]

    def attend(chunk):
        state[:] = attend_chunk(
            queries,
            held[chunk],
            sources,
            place.reshape(1),
            pattern,
            keep,
            firsts[chunk],
            CHUNKS[chunk],
            total,
            state[0],
        )

    climb((0, 0))
    climb((1, 0))
    climb((2, 0), (0, stride))
    climb((3, 0), (1, stride))
    climb((2, stride), (3, stride))
    tokens = {}
    waits = {
        (2, near): lambda: [tokens[0]],
        (3, distances[0]): lambda: [tokens[0]],
        (3, nearest): lambda: [tokens[1]],
    }
    for chunk in chunks:
        for distance in distances:
            if (chunk, distance) == (3, nearest):
                attend(1)
                tokens[1] = state[1]
            swap(chunk, distance, *waits.get((chunk, distance), list)())
            if (chunk, distance) == (0, nearest):
                attend(0)
                tokens[0] = state[1]
    attend(2)
    attend(3)
    return state[0]


def solution(mesh):
    return jax.shard_map(
        body,
        mesh=mesh,
        in_specs=(P(AXES, None), P(AXES, None), P(AXES, None), P(), P()),
        out_specs=P(AXES, None),
        check_vma=False,
    )
```

```python
import functools
import math

import jax
import jax.numpy as jnp
from jax import lax
from jax.experimental import pallas as pl
from jax.experimental.pallas import tpu as pltpu
from jax.sharding import PartitionSpec as P

QUERY_HEADS = 64
KEY_VALUE_HEADS = 8
HEAD_SIZE = 128
BLOCK_TOKENS = 128
GROUP = QUERY_HEADS // KEY_VALUE_HEADS
AXES = ("seq", "head")
CHUNKS = (2, 2, 2, 2)
ROW_HEADS = 2
STEP_BLOCKS = 2
MASKED = -1e30
SCALE = math.log2(math.e) / math.sqrt(HEAD_SIZE)
PRODUCTS = (3, 6)
LIMIT = 32.0
SQUARINGS = 7
QUADRATIC, CUBIC = 0.50101449, 0.16668129
LEAST_SUM = 2.0**-8
GREATEST_SUM = 2.0**30


def power_by_products(scores):
    unit = SCALE * math.log(2.0) / 2**SQUARINGS
    x = jnp.maximum(scores, -LIMIT / SCALE)
    value = 1.0 + x * (unit + x * (QUADRATIC * unit**2 + x * (CUBIC * unit**3)))
    for _ in range(SQUARINGS):
        value = value * value
    return value


def attend_kernel(levels, blocks, parts, sources, place_ref, pattern_ref, keep_ref, q_ref, *refs):
    count = len(sources)
    k_refs, v_refs = refs[:count], refs[count : 2 * count]
    out_ref, token_ref = refs[-2:]
    first = place_ref[0] * blocks

    def pick(source, local):
        local = jnp.clip(local, 0, blocks - 1)
        rows = pl.ds(pl.multiple_of(local * BLOCK_TOKENS, BLOCK_TOKENS), BLOCK_TOKENS)
        return k_refs[source][rows, :], v_refs[source][rows, :]

    def gather(block):
        k_part, v_part = pick(0, block)
        ones = jnp.ones_like(v_part)
        k_parts, v_parts, lives = [k_part], [jnp.concatenate([v_part, ones], 1)], []
        for level in range(levels):
            span = 2**level
            named = pattern_ref[first + block, level]
            if span < blocks:
                local = named - first
                near_k, near_v = pick(0, local)
                far_k, far_v = pick(sources.index(1), local + blocks)
                k_part = jnp.where(local >= 0, near_k, far_k)
                v_part = jnp.where(local >= 0, near_v, far_v)
            else:
                shift = span // blocks
                k_part, v_part = pick(sources.index(shift), named - first + shift * blocks)
            live = keep_ref[first + block, level] > 0
            factor = jnp.where(live, 1.0, 0.0).astype(jnp.bfloat16)
            k_parts.append(k_part * factor)
            v_parts.append(jnp.concatenate([v_part * factor, ones * factor], 1))
            lives.append(live)
        return jnp.concatenate(k_parts, 0), jnp.concatenate(v_parts, 0), lives

    def query_rows(part, heads):
        rows = slice(part * BLOCK_TOKENS, (part + 1) * BLOCK_TOKENS)
        return jnp.concatenate(
            [q_ref[rows, h * HEAD_SIZE : (h + 1) * HEAD_SIZE] for h in heads], 0
        )

    def score(q, k):
        return lax.dot_general(
            q, k, (((1,), (1,)), ((), ())), preferred_element_type=jnp.float32
        )

    def store(part, heads, sums):
        total = sums[:, HEAD_SIZE:]
        inverse = pl.reciprocal(total, approx=True)
        inverse = inverse * (2.0 - total * inverse)
        result = (sums[:, :HEAD_SIZE] * inverse).astype(jnp.bfloat16)
        rows = slice(part * BLOCK_TOKENS, (part + 1) * BLOCK_TOKENS)
        for at, h in enumerate(heads):
            out_ref[rows, h * HEAD_SIZE : (h + 1) * HEAD_SIZE] = result[
                at * BLOCK_TOKENS : (at + 1) * BLOCK_TOKENS
            ]

    def causal_of(heads):
        shape = (heads * BLOCK_TOKENS, BLOCK_TOKENS)
        token = lax.broadcasted_iota(jnp.int32, shape, 0) % BLOCK_TOKENS
        return token >= lax.broadcasted_iota(jnp.int32, shape, 1)

    here = pl.program_id(1) * parts

    def quick():
        gathered = [gather(here + part) for part in range(parts)]
        steps = [
            (part, range(h, h + ROW_HEADS))
            for part in range(parts)
            for h in range(0, GROUP, ROW_HEADS)
        ]
        causal = causal_of(ROW_HEADS)

        def scores_of(step):
            part, heads = step
            return score(query_rows(part, heads), gathered[part][0])

        least = jnp.full((8, HEAD_SIZE), GREATEST_SUM, jnp.float32)
        greatest = jnp.full((8, HEAD_SIZE), LEAST_SUM, jnp.float32)
        ahead = scores_of(steps[0])
        for at, (part, heads) in enumerate(steps):
            scores = ahead
            if at + 1 < len(steps):
                ahead = scores_of(steps[at + 1])
            weights = []
            for slot in range(levels + 1):
                part_scores = scores[:, slot * BLOCK_TOKENS : (slot + 1) * BLOCK_TOKENS]
                if slot in PRODUCTS:
                    weight = power_by_products(part_scores)
                else:
                    weight = jnp.exp2(part_scores * SCALE)
                if slot == 0:
                    weight = jnp.where(causal, weight, 0.0)
                weights.append(weight.astype(jnp.bfloat16))
            weights = jnp.concatenate(weights, 1)
            sums = jnp.dot(weights, gathered[part][1], preferred_element_type=jnp.float32)
            store(part, heads, sums)
            total = sums[:, HEAD_SIZE:].reshape(-1, 8, HEAD_SIZE)
            least = jnp.minimum(least, jnp.min(total, axis=0))
            greatest = jnp.maximum(greatest, jnp.max(total, axis=0))
        return least, greatest

    def careful():
        for part in range(parts):
            k, v, lives = gather(here + part)
            bias = jnp.concatenate(
                [
                    jnp.full((1, BLOCK_TOKENS), jnp.where(live, 0.0, MASKED), jnp.float32)
                    for live in lives
                ],
                1,
            )
            causal = causal_of(1)
            for h in range(GROUP):
                scores = score(query_rows(part, [h]), k)
                diag = jnp.where(causal, scores[:, :BLOCK_TOKENS], MASKED)
                scores = jnp.concatenate([diag, scores[:, BLOCK_TOKENS:] + bias], 1)
                peak = jnp.max(scores, axis=1, keepdims=True)
                weights = jnp.exp2((scores - peak) * SCALE).astype(jnp.bfloat16)
                store(part, [h], jnp.dot(weights, v, preferred_element_type=jnp.float32))

    token_ref[0] = 0
    least, greatest = quick()
    fine = (jnp.min(least) > LEAST_SUM) & (jnp.max(greatest) < GREATEST_SUM)
    pl.when(jnp.logical_not(fine))(careful)


def attend_chunk(queries, held, sources, place, pattern, keep, first_head, heads, total, out):
    rows, width = queries.shape
    blocks = rows // BLOCK_TOKENS
    levels = (blocks * total - 1).bit_length()
    group_width = GROUP * HEAD_SIZE

    parts = math.gcd(blocks, STEP_BLOCKS)
    q_block = (parts * BLOCK_TOKENS, group_width)

    def q_index(head, step, *_):
        return step, first_head + head

    in_specs = [pl.BlockSpec(q_block, q_index)]
    operands = [queries]
    for offset in (0, heads):
        for source in sources:
            array, column = held[source]
            in_specs.append(
                pl.BlockSpec(
                    (rows, HEAD_SIZE), lambda head, step, *_, o=column + offset: (0, o + head)
                )
            )
            operands.append(array)
    aliases = {}
    if out is not None:
        in_specs.append(pl.BlockSpec(memory_space=pl.ANY))
        aliases = {3 + len(operands): 0}
        operands.append(out)
    return pl.pallas_call(
        functools.partial(attend_kernel, levels, blocks, parts, sources),
        grid_spec=pltpu.PrefetchScalarGridSpec(
            num_scalar_prefetch=3,
            grid=(heads, blocks // parts),
            in_specs=in_specs,
            out_specs=[
                pl.BlockSpec(q_block, q_index),
                pl.BlockSpec(memory_space=pltpu.SMEM),
            ],
        ),
        out_shape=[
            jax.ShapeDtypeStruct((rows, width), jnp.bfloat16),
            jax.ShapeDtypeStruct((1,), jnp.int32),
        ],
        input_output_aliases=aliases,
        compiler_params=pltpu.CompilerParams(vmem_limit_bytes=44 * 2**20),
        cost_estimate=pl.CostEstimate(
            flops=5000000000,
            bytes_accessed=1,
            transcendentals=1,
        ),
    )(place, pattern, keep, *operands)


def zero_after(*others):
    total = jnp.int32(0)
    for other in others:
        if jnp.issubdtype(other.dtype, jnp.integer):
            total += other.reshape(-1)[0]
        else:
            corner = other[0, 0].astype(jnp.float32)
            total += (corner != corner).astype(jnp.int32)
    return total


def body(queries, keys, values, pattern, keep):
    total = lax.axis_size(AXES)
    place = lax.axis_index(AXES).astype(jnp.int32)
    sources = tuple([0] + [2**b for b in range(total.bit_length() - 1)])
    stride = max(total // 4, 1)
    up = [(p, p + stride) for p in range(total - stride)]
    chunks = range(len(CHUNKS))
    distances = [stride >> k for k in range(1, stride.bit_length())]
    near, nearest = distances[1], distances[-1]
    firsts = [sum(CHUNKS[:c]) for c in chunks]
    held = []
    for first, heads in zip(firsts, CHUNKS):
        columns = slice(first * HEAD_SIZE, (first + heads) * HEAD_SIZE)
        kv = jnp.concatenate([keys[:, columns], values[:, columns]], 1)
        held.append({0: (lax.optimization_barrier(kv), 0)})

    def part_of(chunk, source):
        array, column = held[chunk][source]
        width = 2 * CHUNKS[chunk] * HEAD_SIZE
        return array[:, column * HEAD_SIZE : column * HEAD_SIZE + width]

    def climb(*moves):
        sent = jnp.concatenate([part_of(*move) for move in moves], 1)
        arrived, column = lax.ppermute(sent, AXES, up), 0
        for chunk, source in moves:
            held[chunk][source + stride] = arrived, column
            column += 2 * CHUNKS[chunk]

    def swap(chunk, distance, *others):
        upper = (place & distance) > zero_after(*others)
        sent = jnp.where(upper, part_of(chunk, 2 * distance), part_of(chunk, 0))
        pairs = [(p, p ^ distance) for p in range(total)]
        held[chunk][distance] = lax.ppermute(sent, AXES, pairs), 0

    state = [None, None]

    def attend(chunk):
        state[:] = attend_chunk(
            queries,
            held[chunk],
            sources,
            place.reshape(1),
            pattern,
            keep,
            firsts[chunk],
            CHUNKS[chunk],
            total,
            state[0],
        )

    climb((0, 0))
    climb((1, 0))
    climb((2, 0), (0, stride))
    climb((3, 0), (1, stride))
    climb((2, stride), (3, stride))
    tokens = {}
    waits = {
        (2, near): lambda: [tokens[0]],
        (3, distances[0]): lambda: [tokens[0]],
        (3, nearest): lambda: [tokens[1]],
    }
    for chunk in chunks:
        for distance in distances:
            if (chunk, distance) == (3, nearest):
                attend(1)
                tokens[1] = state[1]
            swap(chunk, distance, *waits.get((chunk, distance), list)())
            if (chunk, distance) == (0, nearest):
                attend(0)
                tokens[0] = state[1]
    attend(2)
    attend(3)
    return state[0]


def solution(mesh):
    return jax.shard_map(
        body,
        mesh=mesh,
        in_specs=(P(AXES, None), P(AXES, None), P(AXES, None), P(), P()),
        out_specs=P(AXES, None),
        check_vma=False,
    )
```

```python
import functools
import math

import jax
import jax.numpy as jnp
from jax import lax
from jax.experimental import pallas as pl
from jax.experimental.pallas import tpu as pltpu
from jax.sharding import PartitionSpec as P

QUERY_HEADS = 64
KEY_VALUE_HEADS = 8
HEAD_SIZE = 128
BLOCK_TOKENS = 128
GROUP = QUERY_HEADS // KEY_VALUE_HEADS
AXES = ("seq", "head")
CHUNKS = (2, 2, 2, 2)
ROW_HEADS = 2
TILE_SLOTS = 2
STEP_BLOCKS = 2
MASKED = -1e30
SCALE = math.log2(math.e) / math.sqrt(HEAD_SIZE)
LEAST_SUM = 1e-25
GREATEST_SUM = 1e30


def attend_kernel(levels, blocks, parts, sources, place_ref, pattern_ref, keep_ref, q_ref, *refs):
    count = len(sources)
    k_refs, v_refs = refs[:count], refs[count : 2 * count]
    out_ref, token_ref = refs[-2:]
    first = place_ref[0] * blocks

    def pick(source, local):
        local = jnp.clip(local, 0, blocks - 1)
        rows = pl.ds(pl.multiple_of(local * BLOCK_TOKENS, BLOCK_TOKENS), BLOCK_TOKENS)
        return k_refs[source][rows, :], v_refs[source][rows, :]

    def gather(block):
        k_part, v_part = pick(0, block)
        ones = jnp.ones_like(v_part)
        k_parts, v_parts, lives = [k_part], [jnp.concatenate([v_part, ones], 1)], []
        for level in range(levels):
            span = 2**level
            named = pattern_ref[first + block, level]
            if span < blocks:
                local = named - first
                near_k, near_v = pick(0, local)
                far_k, far_v = pick(sources.index(1), local + blocks)
                k_part = jnp.where(local >= 0, near_k, far_k)
                v_part = jnp.where(local >= 0, near_v, far_v)
            else:
                shift = span // blocks
                k_part, v_part = pick(sources.index(shift), named - first + shift * blocks)
            live = keep_ref[first + block, level] > 0
            factor = jnp.where(live, 1.0, 0.0).astype(jnp.bfloat16)
            k_parts.append(k_part * factor)
            v_parts.append(jnp.concatenate([v_part * factor, ones * factor], 1))
            lives.append(live)
        return jnp.concatenate(k_parts, 0), jnp.concatenate(v_parts, 0), lives

    def query_rows(part, heads):
        rows = slice(part * BLOCK_TOKENS, (part + 1) * BLOCK_TOKENS)
        return jnp.concatenate(
            [q_ref[rows, h * HEAD_SIZE : (h + 1) * HEAD_SIZE] for h in heads], 0
        )

    def score(q, k):
        return lax.dot_general(
            q, k, (((1,), (1,)), ((), ())), preferred_element_type=jnp.float32
        )

    def store(part, heads, sums):
        total = sums[:, HEAD_SIZE:]
        inverse = pl.reciprocal(total, approx=True)
        inverse = inverse * (2.0 - total * inverse)
        result = (sums[:, :HEAD_SIZE] * inverse).astype(jnp.bfloat16)
        rows = slice(part * BLOCK_TOKENS, (part + 1) * BLOCK_TOKENS)
        for at, h in enumerate(heads):
            out_ref[rows, h * HEAD_SIZE : (h + 1) * HEAD_SIZE] = result[
                at * BLOCK_TOKENS : (at + 1) * BLOCK_TOKENS
            ]

    def causal_of(heads):
        shape = (heads * BLOCK_TOKENS, BLOCK_TOKENS)
        token = lax.broadcasted_iota(jnp.int32, shape, 0) % BLOCK_TOKENS
        return token >= lax.broadcasted_iota(jnp.int32, shape, 1)

    here = pl.program_id(1) * parts

    def quick():
        gathered = [gather(here + part) for part in range(parts)]
        steps = [
            (part, range(h, h + ROW_HEADS))
            for part in range(parts)
            for h in range(0, GROUP, ROW_HEADS)
        ]
        causal = causal_of(ROW_HEADS)

        count_of = levels + 1
        tiles = [
            slice(t * BLOCK_TOKENS, min(t + TILE_SLOTS, count_of) * BLOCK_TOKENS)
            for t in range(0, count_of, TILE_SLOTS)
        ]
        least = jnp.full((8, HEAD_SIZE), GREATEST_SUM, jnp.float32)
        greatest = jnp.full((8, HEAD_SIZE), LEAST_SUM, jnp.float32)
        pieces = [(part, heads, t) for part, heads in steps for t in range(len(tiles))]

        def scores_of(piece):
            part, heads, t = piece
            return score(query_rows(part, heads), gathered[part][0][tiles[t]])

        def weights_of(piece, scores):
            weights = jnp.exp2(scores * SCALE)
            if piece[2] == 0:
                diag = jnp.where(causal, weights[:, :BLOCK_TOKENS], 0.0)
                weights = jnp.concatenate([diag, weights[:, BLOCK_TOKENS:]], 1)
            return weights.astype(jnp.bfloat16)

        def product_of(piece, weights):
            part, _, t = piece
            return jnp.dot(weights, gathered[part][1][tiles[t]], preferred_element_type=jnp.float32)

        ahead = [scores_of(piece) for piece in pieces[:2]]
        behind, sums = None, None
        for at in range(len(pieces) + 1):
            if at + 2 < len(pieces):
                ahead.append(scores_of(pieces[at + 2]))
            weights = None
            if at < len(pieces):
                weights = weights_of(pieces[at], ahead.pop(0))
            if behind is not None:
                part, heads, t = pieces[at - 1]
                product = product_of(pieces[at - 1], behind)
                sums = product if t == 0 else sums + product
                if t == len(tiles) - 1:
                    store(part, heads, sums)
                    total = sums[:, HEAD_SIZE:].reshape(-1, 8, HEAD_SIZE)
                    least = jnp.minimum(least, jnp.min(total, axis=0))
                    greatest = jnp.maximum(greatest, jnp.max(total, axis=0))
            behind = weights
        return least, greatest

    def careful():
        for part in range(parts):
            k, v, lives = gather(here + part)
            bias = jnp.concatenate(
                [
                    jnp.full((1, BLOCK_TOKENS), jnp.where(live, 0.0, MASKED), jnp.float32)
                    for live in lives
                ],
                1,
            )
            causal = causal_of(1)
            for h in range(GROUP):
                scores = score(query_rows(part, [h]), k)
                diag = jnp.where(causal, scores[:, :BLOCK_TOKENS], MASKED)
                scores = jnp.concatenate([diag, scores[:, BLOCK_TOKENS:] + bias], 1)
                peak = jnp.max(scores, axis=1, keepdims=True)
                weights = jnp.exp2((scores - peak) * SCALE).astype(jnp.bfloat16)
                store(part, [h], jnp.dot(weights, v, preferred_element_type=jnp.float32))

    token_ref[0] = 0
    least, greatest = quick()
    fine = (jnp.min(least) > LEAST_SUM) & (jnp.max(greatest) < GREATEST_SUM)
    pl.when(jnp.logical_not(fine))(careful)


def attend_chunk(queries, held, sources, place, pattern, keep, first_head, heads, total, out, waited):
    rows, width = queries.shape
    blocks = rows // BLOCK_TOKENS
    levels = (blocks * total - 1).bit_length()
    group_width = GROUP * HEAD_SIZE

    parts = math.gcd(blocks, STEP_BLOCKS)
    q_block = (parts * BLOCK_TOKENS, group_width)

    def q_index(head, step, *_):
        return step, first_head + head

    in_specs = [pl.BlockSpec(q_block, q_index)]
    operands = [queries]
    for offset in (0, heads):
        for source in sources:
            array, column = held[source]
            in_specs.append(
                pl.BlockSpec(
                    (rows, HEAD_SIZE), lambda head, step, *_, o=column + offset: (0, o + head)
                )
            )
            operands.append(array)
    for array in waited:
        in_specs.append(pl.BlockSpec(memory_space=pl.ANY))
        operands.append(array)
    aliases = {}
    if out is not None:
        in_specs.append(pl.BlockSpec(memory_space=pl.ANY))
        aliases = {3 + len(operands): 0}
        operands.append(out)
    return pl.pallas_call(
        functools.partial(attend_kernel, levels, blocks, parts, sources),
        grid_spec=pltpu.PrefetchScalarGridSpec(
            num_scalar_prefetch=3,
            grid=(heads, blocks // parts),
            in_specs=in_specs,
            out_specs=[
                pl.BlockSpec(q_block, q_index),
                pl.BlockSpec(memory_space=pltpu.SMEM),
            ],
        ),
        out_shape=[
            jax.ShapeDtypeStruct((rows, width), jnp.bfloat16),
            jax.ShapeDtypeStruct((1,), jnp.int32),
        ],
        input_output_aliases=aliases,
        compiler_params=pltpu.CompilerParams(vmem_limit_bytes=44 * 2**20),
        cost_estimate=pl.CostEstimate(
            flops=1,
            bytes_accessed=1,
            transcendentals=1,
        ),
    )(place, pattern, keep, *operands)


def zero_after(*others):
    total = jnp.int32(0)
    for other in others:
        if jnp.issubdtype(other.dtype, jnp.integer):
            total += other.reshape(-1)[0]
        else:
            corner = other[0, 0].astype(jnp.float32)
            total += (corner != corner).astype(jnp.int32)
    return total


def body(queries, keys, values, pattern, keep):
    total = lax.axis_size(AXES)
    place = lax.axis_index(AXES).astype(jnp.int32)
    sources = tuple([0] + [2**b for b in range(total.bit_length() - 1)])
    stride = max(total // 4, 1)
    up = [(p, p + stride) for p in range(total - stride)]
    chunks = range(len(CHUNKS))
    distances = [stride >> k for k in range(1, stride.bit_length())]
    near, nearest = distances[1], distances[-1]
    firsts = [sum(CHUNKS[:c]) for c in chunks]
    held = []
    for first, heads in zip(firsts, CHUNKS):
        columns = slice(first * HEAD_SIZE, (first + heads) * HEAD_SIZE)
        kv = jnp.concatenate([keys[:, columns], values[:, columns]], 1)
        held.append({0: (lax.optimization_barrier(kv), 0)})

    def part_of(chunk, source):
        array, column = held[chunk][source]
        width = 2 * CHUNKS[chunk] * HEAD_SIZE
        return array[:, column * HEAD_SIZE : column * HEAD_SIZE + width]

    def climb(*moves):
        sent = jnp.concatenate([part_of(*move) for move in moves], 1)
        arrived, column = lax.ppermute(sent, AXES, up), 0
        for chunk, source in moves:
            held[chunk][source + stride] = arrived, column
            column += 2 * CHUNKS[chunk]

    def swap(chunk, distance, *others):
        upper = (place & distance) > zero_after(*others)
        sent = jnp.where(upper, part_of(chunk, 2 * distance), part_of(chunk, 0))
        pairs = [(p, p ^ distance) for p in range(total)]
        held[chunk][distance] = lax.ppermute(sent, AXES, pairs), 0

    state = [None, None]

    def attend(chunk, *waited):
        state[:] = attend_chunk(
            queries,
            held[chunk],
            sources,
            place.reshape(1),
            pattern,
            keep,
            firsts[chunk],
            CHUNKS[chunk],
            total,
            state[0],
            waited,
        )

    climb((0, 0))
    climb((1, 0))
    climb((2, 0), (0, stride))
    climb((3, 0), (1, stride))
    climb((2, stride))
    climb((3, stride))
    tokens = {}
    waits = {
        (2, near): lambda: [tokens[0]],
        (3, distances[0]): lambda: [tokens[0]],
        (2, nearest): lambda: [tokens[1]],
        (3, near): lambda: [tokens[1], part_of(2, 2 * stride)],
        (3, nearest): lambda: [tokens[2]],
    }
    for chunk in (0, 1):
        for distance in distances:
            swap(chunk, distance)
    attend(0, held[1][nearest][0])
    tokens[0] = state[1]
    attend(1)
    tokens[1] = state[1]
    for chunk in (2, 3):
        for distance in distances:
            if (chunk, distance) == (3, nearest):
                attend(2)
                tokens[2] = state[1]
            swap(chunk, distance, *waits.get((chunk, distance), list)())
    attend(3)
    return state[0]


def solution(mesh):
    return jax.shard_map(
        body,
        mesh=mesh,
        in_specs=(P(AXES, None), P(AXES, None), P(AXES, None), P(), P()),
        out_specs=P(AXES, None),
        check_vma=False,
    )
```

```python
import functools
import math

import jax
import jax.numpy as jnp
from jax import lax
from jax.experimental import pallas as pl
from jax.experimental.pallas import tpu as pltpu
from jax.sharding import PartitionSpec as P

QUERY_HEADS = 64
KEY_VALUE_HEADS = 8
HEAD_SIZE = 128
BLOCK_TOKENS = 128
GROUP = QUERY_HEADS // KEY_VALUE_HEADS
AXES = ("seq", "head")
CHUNKS = (2, 2, 2, 2)
ROW_HEADS = 2
TILE_SLOTS = 2
STEP_BLOCKS = 2
MASKED = -1e30
SCALE = math.log2(math.e) / math.sqrt(HEAD_SIZE)
LEAST_SUM = 1e-25
GREATEST_SUM = 1e30


def attend_kernel(
    levels, blocks, parts, sources, columns, heads_held, place_ref, pattern_ref, keep_ref, q_ref, *refs
):
    count = len(sources)
    kv_refs = refs[:count]
    out_ref, token_ref = refs[-2:]
    first = place_ref[0] * blocks

    def pick(source, local):
        local = jnp.clip(local, 0, blocks - 1)
        rows = pl.ds(pl.multiple_of(local * BLOCK_TOKENS, BLOCK_TOKENS), BLOCK_TOKENS)
        start = (columns[source] + pl.program_id(0)) * HEAD_SIZE
        k_columns = pl.ds(pl.multiple_of(start, HEAD_SIZE), HEAD_SIZE)
        v_columns = pl.ds(pl.multiple_of(start + heads_held * HEAD_SIZE, HEAD_SIZE), HEAD_SIZE)
        return kv_refs[source][rows, k_columns], kv_refs[source][rows, v_columns]

    def gather(block):
        k_part, v_part = pick(0, block)
        ones = jnp.ones_like(v_part)
        k_parts, v_parts, lives = [k_part], [jnp.concatenate([v_part, ones], 1)], []
        for level in range(levels):
            span = 2**level
            named = pattern_ref[first + block, level]
            if span < blocks:
                local = named - first
                near_k, near_v = pick(0, local)
                far_k, far_v = pick(sources.index(1), local + blocks)
                k_part = jnp.where(local >= 0, near_k, far_k)
                v_part = jnp.where(local >= 0, near_v, far_v)
            else:
                shift = span // blocks
                k_part, v_part = pick(sources.index(shift), named - first + shift * blocks)
            live = keep_ref[first + block, level] > 0
            factor = jnp.where(live, 1.0, 0.0).astype(jnp.bfloat16)
            k_parts.append(k_part * factor)
            v_parts.append(jnp.concatenate([v_part * factor, ones * factor], 1))
            lives.append(live)
        return jnp.concatenate(k_parts, 0), jnp.concatenate(v_parts, 0), lives

    def query_rows(part, heads):
        rows = slice(part * BLOCK_TOKENS, (part + 1) * BLOCK_TOKENS)
        return jnp.concatenate(
            [q_ref[rows, h * HEAD_SIZE : (h + 1) * HEAD_SIZE] for h in heads], 0
        )

    def score(q, k):
        return lax.dot_general(
            q, k, (((1,), (1,)), ((), ())), preferred_element_type=jnp.float32
        )

    def store(part, heads, sums):
        total = sums[:, HEAD_SIZE:]
        inverse = pl.reciprocal(total, approx=True)
        inverse = inverse * (2.0 - total * inverse)
        result = (sums[:, :HEAD_SIZE] * inverse).astype(jnp.bfloat16)
        rows = slice(part * BLOCK_TOKENS, (part + 1) * BLOCK_TOKENS)
        for at, h in enumerate(heads):
            out_ref[rows, h * HEAD_SIZE : (h + 1) * HEAD_SIZE] = result[
                at * BLOCK_TOKENS : (at + 1) * BLOCK_TOKENS
            ]

    def causal_of(heads):
        shape = (heads * BLOCK_TOKENS, BLOCK_TOKENS)
        token = lax.broadcasted_iota(jnp.int32, shape, 0) % BLOCK_TOKENS
        return token >= lax.broadcasted_iota(jnp.int32, shape, 1)

    here = pl.program_id(1) * parts

    def quick():
        gathered = [gather(here + part) for part in range(parts)]
        steps = [
            (part, range(h, h + ROW_HEADS))
            for part in range(parts)
            for h in range(0, GROUP, ROW_HEADS)
        ]
        causal = causal_of(ROW_HEADS)

        count_of = levels + 1
        tiles = [
            slice(t * BLOCK_TOKENS, min(t + TILE_SLOTS, count_of) * BLOCK_TOKENS)
            for t in range(0, count_of, TILE_SLOTS)
        ]
        least = jnp.full((8, HEAD_SIZE), GREATEST_SUM, jnp.float32)
        greatest = jnp.full((8, HEAD_SIZE), LEAST_SUM, jnp.float32)
        pieces = [(part, heads, t) for part, heads in steps for t in range(len(tiles))]

        def scores_of(piece):
            part, heads, t = piece
            return score(query_rows(part, heads), gathered[part][0][tiles[t]])

        def weights_of(piece, scores):
            weights = jnp.exp2(scores * SCALE)
            if piece[2] == 0:
                diag = jnp.where(causal, weights[:, :BLOCK_TOKENS], 0.0)
                weights = jnp.concatenate([diag, weights[:, BLOCK_TOKENS:]], 1)
            return weights.astype(jnp.bfloat16)

        def product_of(piece, weights):
            part, _, t = piece
            return jnp.dot(weights, gathered[part][1][tiles[t]], preferred_element_type=jnp.float32)

        ahead = [scores_of(piece) for piece in pieces[:2]]
        behind, sums = None, None
        for at in range(len(pieces) + 1):
            if at + 2 < len(pieces):
                ahead.append(scores_of(pieces[at + 2]))
            weights = None
            if at < len(pieces):
                weights = weights_of(pieces[at], ahead.pop(0))
            if behind is not None:
                part, heads, t = pieces[at - 1]
                product = product_of(pieces[at - 1], behind)
                sums = product if t == 0 else sums + product
                if t == len(tiles) - 1:
                    store(part, heads, sums)
                    total = sums[:, HEAD_SIZE:].reshape(-1, 8, HEAD_SIZE)
                    least = jnp.minimum(least, jnp.min(total, axis=0))
                    greatest = jnp.maximum(greatest, jnp.max(total, axis=0))
            behind = weights
        return least, greatest

    def careful():
        for part in range(parts):
            k, v, lives = gather(here + part)
            bias = jnp.concatenate(
                [
                    jnp.full((1, BLOCK_TOKENS), jnp.where(live, 0.0, MASKED), jnp.float32)
                    for live in lives
                ],
                1,
            )
            causal = causal_of(1)
            for h in range(GROUP):
                scores = score(query_rows(part, [h]), k)
                diag = jnp.where(causal, scores[:, :BLOCK_TOKENS], MASKED)
                scores = jnp.concatenate([diag, scores[:, BLOCK_TOKENS:] + bias], 1)
                peak = jnp.max(scores, axis=1, keepdims=True)
                weights = jnp.exp2((scores - peak) * SCALE).astype(jnp.bfloat16)
                store(part, [h], jnp.dot(weights, v, preferred_element_type=jnp.float32))

    token_ref[0] = 0
    least, greatest = quick()
    fine = (jnp.min(least) > LEAST_SUM) & (jnp.max(greatest) < GREATEST_SUM)
    pl.when(jnp.logical_not(fine))(careful)


def attend_chunk(queries, held, sources, place, pattern, keep, first_head, heads, total, out, waited):
    rows, width = queries.shape
    blocks = rows // BLOCK_TOKENS
    levels = (blocks * total - 1).bit_length()
    group_width = GROUP * HEAD_SIZE

    parts = math.gcd(blocks, STEP_BLOCKS)
    q_block = (parts * BLOCK_TOKENS, group_width)

    def q_index(head, step, *_):
        return step, first_head + head

    in_specs = [pl.BlockSpec(q_block, q_index)]
    operands = [queries]
    for source in sources:
        in_specs.append(pl.BlockSpec(memory_space=pltpu.VMEM))
        operands.append(held[source][0])
    columns = [held[source][1] for source in sources]
    for array in waited:
        in_specs.append(pl.BlockSpec(memory_space=pl.ANY))
        operands.append(array)
    aliases = {}
    if out is not None:
        in_specs.append(pl.BlockSpec(memory_space=pl.ANY))
        aliases = {3 + len(operands): 0}
        operands.append(out)
    return pl.pallas_call(
        functools.partial(attend_kernel, levels, blocks, parts, sources, columns, heads),
        grid_spec=pltpu.PrefetchScalarGridSpec(
            num_scalar_prefetch=3,
            grid=(heads, blocks // parts),
            in_specs=in_specs,
            out_specs=[
                pl.BlockSpec(q_block, q_index),
                pl.BlockSpec(memory_space=pltpu.SMEM),
            ],
        ),
        out_shape=[
            jax.ShapeDtypeStruct((rows, width), jnp.bfloat16),
            jax.ShapeDtypeStruct((1,), jnp.int32),
        ],
        input_output_aliases=aliases,
        compiler_params=pltpu.CompilerParams(vmem_limit_bytes=26 * 2**20),
        cost_estimate=pl.CostEstimate(
            flops=1,
            bytes_accessed=1,
            transcendentals=1,
        ),
    )(place, pattern, keep, *operands)


def body(queries, keys, values, pattern, keep):
    total = lax.axis_size(AXES)
    place = lax.axis_index(AXES).astype(jnp.int32)
    sources = tuple([0] + [2**b for b in range(total.bit_length() - 1)])
    stride = max(total // 4, 1)
    up = [(p, p + stride) for p in range(total - stride)]
    chunks = range(len(CHUNKS))
    distances = [stride >> k for k in range(1, stride.bit_length())]
    near, nearest = distances[1], distances[-1]
    firsts = [sum(CHUNKS[:c]) for c in chunks]
    held = []
    for first, heads in zip(firsts, CHUNKS):
        columns = slice(first * HEAD_SIZE, (first + heads) * HEAD_SIZE)
        kv = jnp.concatenate([keys[:, columns], values[:, columns]], 1)
        held.append({0: (lax.optimization_barrier(kv), 0)})

    def part_of(chunk, source):
        array, column = held[chunk][source]
        width = 2 * CHUNKS[chunk] * HEAD_SIZE
        return array[:, column * HEAD_SIZE : column * HEAD_SIZE + width]

    def climb(*moves):
        sent = jnp.concatenate([part_of(*move) for move in moves], 1)
        arrived, column = lax.ppermute(sent, AXES, up), 0
        for chunk, source in moves:
            held[chunk][source + stride] = arrived, column
            column += 2 * CHUNKS[chunk]

    def swap(chunk, distance, token=None, other=None):
        upper = (place & distance) > (0 if token is None else token[0])
        sent = jnp.where(upper, part_of(chunk, 2 * distance), part_of(chunk, 0))
        if other is not None:
            sent = jnp.where(other != other, other, sent)
        pairs = [(p, p ^ distance) for p in range(total)]
        held[chunk][distance] = lax.ppermute(sent, AXES, pairs), 0

    state = [None, None]

    def attend(chunk, *waited):
        state[:] = attend_chunk(
            queries,
            held[chunk],
            sources,
            place.reshape(1),
            pattern,
            keep,
            firsts[chunk],
            CHUNKS[chunk],
            total,
            state[0],
            waited,
        )

    climb((0, 0))
    climb((1, 0))
    climb((2, 0), (0, stride))
    climb((3, 0), (1, stride))
    climb((2, stride))
    climb((3, stride))
    tokens = {}
    waits = {
        (2, near): lambda: [tokens[0]],
        (3, distances[0]): lambda: [tokens[0]],
        (2, nearest): lambda: [tokens[1]],
        (3, near): lambda: [tokens[1], part_of(2, 2 * stride)],
        (3, nearest): lambda: [tokens[2]],
    }
    for chunk in (0, 1):
        for distance in distances:
            swap(chunk, distance)
    attend(0, held[1][nearest][0])
    tokens[0] = state[1]
    attend(1)
    tokens[1] = state[1]
    for chunk in (2, 3):
        for distance in distances:
            if (chunk, distance) == (3, nearest):
                attend(2)
                tokens[2] = state[1]
            swap(chunk, distance, *waits.get((chunk, distance), list)())
    attend(3)
    return state[0]


def solution(mesh):
    return jax.shard_map(
        body,
        mesh=mesh,
        in_specs=(P(AXES, None), P(AXES, None), P(AXES, None), P(), P()),
        out_specs=P(AXES, None),
        check_vma=False,
    )
```

```python
import functools
import math

import jax
import jax.numpy as jnp
from jax import lax
from jax.experimental import pallas as pl
from jax.experimental.pallas import tpu as pltpu
from jax.sharding import PartitionSpec as P

QUERY_HEADS = 64
KEY_VALUE_HEADS = 8
HEAD_SIZE = 128
BLOCK_TOKENS = 128
GROUP = QUERY_HEADS // KEY_VALUE_HEADS
AXES = ("seq", "head")
CHUNKS = (2, 2, 2, 2)
ROW_HEADS = 2
TILE_SLOTS = 2
STEP_BLOCKS = 2
MASKED = -1e30
SCALE = math.log2(math.e) / math.sqrt(HEAD_SIZE)
LEAST_SUM = 1e-25
GREATEST_SUM = 1e30


def attend_kernel(levels, blocks, parts, sources, place_ref, pattern_ref, keep_ref, q_ref, *refs):
    count = len(sources)
    k_refs, v_refs = refs[:count], refs[count : 2 * count]
    out_ref, token_ref = refs[-2:]
    first = place_ref[0] * blocks

    def pick(source, local):
        local = jnp.clip(local, 0, blocks - 1)
        rows = pl.ds(pl.multiple_of(local * BLOCK_TOKENS, BLOCK_TOKENS), BLOCK_TOKENS)
        return k_refs[source][rows, :], v_refs[source][rows, :]

    def gather(block):
        k_part, v_part = pick(0, block)
        ones = jnp.ones_like(v_part)
        k_parts, v_parts, lives = [k_part], [jnp.concatenate([v_part, ones], 1)], []
        for level in range(levels):
            span = 2**level
            named = pattern_ref[first + block, level]
            if span < blocks:
                local = named - first
                near_k, near_v = pick(0, local)
                far_k, far_v = pick(sources.index(1), local + blocks)
                k_part = jnp.where(local >= 0, near_k, far_k)
                v_part = jnp.where(local >= 0, near_v, far_v)
            else:
                shift = span // blocks
                k_part, v_part = pick(sources.index(shift), named - first + shift * blocks)
            live = keep_ref[first + block, level] > 0
            factor = jnp.where(live, 1.0, 0.0).astype(jnp.bfloat16)
            k_parts.append(k_part * factor)
            v_parts.append(jnp.concatenate([v_part * factor, ones * factor], 1))
            lives.append(live)
        return jnp.concatenate(k_parts, 0), jnp.concatenate(v_parts, 0), lives

    def query_rows(part, heads):
        rows = slice(part * BLOCK_TOKENS, (part + 1) * BLOCK_TOKENS)
        return jnp.concatenate(
            [q_ref[rows, h * HEAD_SIZE : (h + 1) * HEAD_SIZE] for h in heads], 0
        )

    def score(q, k):
        return lax.dot_general(
            q, k, (((1,), (1,)), ((), ())), preferred_element_type=jnp.float32
        )

    def store(part, heads, sums):
        total = sums[:, HEAD_SIZE:]
        inverse = pl.reciprocal(total, approx=True)
        inverse = inverse * (2.0 - total * inverse)
        result = (sums[:, :HEAD_SIZE] * inverse).astype(jnp.bfloat16)
        rows = slice(part * BLOCK_TOKENS, (part + 1) * BLOCK_TOKENS)
        for at, h in enumerate(heads):
            out_ref[rows, h * HEAD_SIZE : (h + 1) * HEAD_SIZE] = result[
                at * BLOCK_TOKENS : (at + 1) * BLOCK_TOKENS
            ]

    def causal_of(heads):
        shape = (heads * BLOCK_TOKENS, BLOCK_TOKENS)
        token = lax.broadcasted_iota(jnp.int32, shape, 0) % BLOCK_TOKENS
        return token >= lax.broadcasted_iota(jnp.int32, shape, 1)

    here = pl.program_id(1) * parts

    def quick():
        gathered = [gather(here + part) for part in range(parts)]
        steps = [
            (part, range(h, h + ROW_HEADS))
            for part in range(parts)
            for h in range(0, GROUP, ROW_HEADS)
        ]
        causal = causal_of(ROW_HEADS)

        count_of = levels + 1
        tiles = [
            slice(t * BLOCK_TOKENS, min(t + TILE_SLOTS, count_of) * BLOCK_TOKENS)
            for t in range(0, count_of, TILE_SLOTS)
        ]
        least = jnp.full((8, HEAD_SIZE), GREATEST_SUM, jnp.float32)
        greatest = jnp.full((8, HEAD_SIZE), LEAST_SUM, jnp.float32)
        pieces = [(part, heads, t) for part, heads in steps for t in range(len(tiles))]

        def scores_of(piece):
            part, heads, t = piece
            return score(query_rows(part, heads), gathered[part][0][tiles[t]])

        def weights_of(piece, scores):
            weights = jnp.exp2(scores * SCALE)
            if piece[2] == 0:
                diag = jnp.where(causal, weights[:, :BLOCK_TOKENS], 0.0)
                weights = jnp.concatenate([diag, weights[:, BLOCK_TOKENS:]], 1)
            return weights.astype(jnp.bfloat16)

        def product_of(piece, weights):
            part, _, t = piece
            return jnp.dot(weights, gathered[part][1][tiles[t]], preferred_element_type=jnp.float32)

        ahead = [scores_of(piece) for piece in pieces[:2]]
        behind, sums = None, None
        for at in range(len(pieces) + 1):
            if at + 2 < len(pieces):
                ahead.append(scores_of(pieces[at + 2]))
            weights = None
            if at < len(pieces):
                weights = weights_of(pieces[at], ahead.pop(0))
            if behind is not None:
                part, heads, t = pieces[at - 1]
                product = product_of(pieces[at - 1], behind)
                sums = product if t == 0 else sums + product
                if t == len(tiles) - 1:
                    store(part, heads, sums)
                    total = sums[:, HEAD_SIZE:].reshape(-1, 8, HEAD_SIZE)
                    least = jnp.minimum(least, jnp.min(total, axis=0))
                    greatest = jnp.maximum(greatest, jnp.max(total, axis=0))
            behind = weights
        return least, greatest

    def careful():
        for part in range(parts):
            k, v, lives = gather(here + part)
            bias = jnp.concatenate(
                [
                    jnp.full((1, BLOCK_TOKENS), jnp.where(live, 0.0, MASKED), jnp.float32)
                    for live in lives
                ],
                1,
            )
            causal = causal_of(1)
            for h in range(GROUP):
                scores = score(query_rows(part, [h]), k)
                diag = jnp.where(causal, scores[:, :BLOCK_TOKENS], MASKED)
                scores = jnp.concatenate([diag, scores[:, BLOCK_TOKENS:] + bias], 1)
                peak = jnp.max(scores, axis=1, keepdims=True)
                weights = jnp.exp2((scores - peak) * SCALE).astype(jnp.bfloat16)
                store(part, [h], jnp.dot(weights, v, preferred_element_type=jnp.float32))

    token_ref[0] = 0
    least, greatest = quick()
    fine = (jnp.min(least) > LEAST_SUM) & (jnp.max(greatest) < GREATEST_SUM)
    pl.when(jnp.logical_not(fine))(careful)


def attend_chunk(queries, held, sources, place, pattern, keep, first_head, heads, total, out, waited):
    rows, width = queries.shape
    blocks = rows // BLOCK_TOKENS
    levels = (blocks * total - 1).bit_length()
    group_width = GROUP * HEAD_SIZE

    parts = math.gcd(blocks, STEP_BLOCKS)
    q_block = (parts * BLOCK_TOKENS, group_width)

    def q_index(head, step, *_):
        return step, first_head + head

    in_specs = [pl.BlockSpec(q_block, q_index)]
    operands = [queries]
    for offset in (0, heads):
        for source in sources:
            array, column = held[source]
            in_specs.append(
                pl.BlockSpec(
                    (rows, HEAD_SIZE), lambda head, step, *_, o=column + offset: (0, o + head)
                )
            )
            operands.append(array)
    for array in waited:
        in_specs.append(pl.BlockSpec(memory_space=pl.ANY))
        operands.append(array)
    aliases = {}
    if out is not None:
        in_specs.append(pl.BlockSpec(memory_space=pl.ANY))
        aliases = {3 + len(operands): 0}
        operands.append(out)
    return pl.pallas_call(
        functools.partial(attend_kernel, levels, blocks, parts, sources),
        grid_spec=pltpu.PrefetchScalarGridSpec(
            num_scalar_prefetch=3,
            grid=(heads, blocks // parts),
            in_specs=in_specs,
            out_specs=[
                pl.BlockSpec(q_block, q_index),
                pl.BlockSpec(memory_space=pltpu.SMEM),
            ],
        ),
        out_shape=[
            jax.ShapeDtypeStruct((rows, width), jnp.bfloat16),
            jax.ShapeDtypeStruct((1,), jnp.int32),
        ],
        input_output_aliases=aliases,
        compiler_params=pltpu.CompilerParams(vmem_limit_bytes=44 * 2**20),
        cost_estimate=pl.CostEstimate(
            flops=1,
            bytes_accessed=1,
            transcendentals=1,
        ),
    )(place, pattern, keep, *operands)


def body(queries, keys, values, pattern, keep):
    total = lax.axis_size(AXES)
    place = lax.axis_index(AXES).astype(jnp.int32)
    sources = tuple([0] + [2**b for b in range(total.bit_length() - 1)])
    stride = max(total // 4, 1)
    up = [(p, p + stride) for p in range(total - stride)]
    chunks = range(len(CHUNKS))
    distances = [stride >> k for k in range(1, stride.bit_length() - 1)]
    nearest = distances[-1]
    firsts = [sum(CHUNKS[:c]) for c in chunks]
    held = []
    for first, heads in zip(firsts, CHUNKS):
        columns = slice(first * HEAD_SIZE, (first + heads) * HEAD_SIZE)
        kv = jnp.concatenate([keys[:, columns], values[:, columns]], 1)
        held.append({0: (lax.optimization_barrier(kv), 0)})

    def part_of(chunk, source):
        array, column = held[chunk][source]
        width = 2 * CHUNKS[chunk] * HEAD_SIZE
        return array[:, column * HEAD_SIZE : column * HEAD_SIZE + width]

    def climb(*moves):
        sent = jnp.concatenate([part_of(*move) for move in moves], 1)
        arrived, column = lax.ppermute(sent, AXES, up), 0
        for chunk, source in moves:
            held[chunk][source + stride] = arrived, column
            column += 2 * CHUNKS[chunk]

    def swap(chunk, distance, token=None, other=None):
        upper = (place & distance) > (0 if token is None else token[0])
        sent = jnp.where(upper, part_of(chunk, 2 * distance), part_of(chunk, 0))
        if other is not None:
            sent = jnp.where(other != other, other, sent)
        pairs = [(p, p ^ distance) for p in range(total)]
        held[chunk][distance] = lax.ppermute(sent, AXES, pairs), 0
        if distance == 2:
            sent = jnp.where((place & 1) > 0, sent, part_of(chunk, 0))
            pairs = [(p, p ^ (3 if p & 1 else 1)) for p in range(total)]
            held[chunk][1] = lax.ppermute(sent, AXES, pairs), 0

    state = [None, None]

    def attend(chunk, *waited):
        state[:] = attend_chunk(
            queries,
            held[chunk],
            sources,
            place.reshape(1),
            pattern,
            keep,
            firsts[chunk],
            CHUNKS[chunk],
            total,
            state[0],
            waited,
        )

    climb((0, 0))
    climb((1, 0))
    climb((2, 0), (0, stride))
    climb((3, 0), (1, stride))
    climb((2, stride))
    climb((3, stride))
    for chunk in (0, 1):
        for distance in distances:
            swap(chunk, distance)
    attend(0)
    token = state[1]
    for distance in distances:
        swap(2, distance, token if distance == nearest else None)
    attend(1, held[2][2][0], held[2][1][0])
    for distance in distances:
        if distance == distances[0]:
            swap(3, distance, token)
        else:
            swap(3, distance, state[1], part_of(2, 2 * stride))
    attend(2)
    attend(3)
    return state[0]


def solution(mesh):
    return jax.shard_map(
        body,
        mesh=mesh,
        in_specs=(P(AXES, None), P(AXES, None), P(AXES, None), P(), P()),
        out_specs=P(AXES, None),
        check_vma=False,
    )
```

```python
import functools
import math

import jax
import jax.numpy as jnp
from jax import lax
from jax.experimental import pallas as pl
from jax.experimental.pallas import tpu as pltpu
from jax.sharding import PartitionSpec as P

QUERY_HEADS = 64
KEY_VALUE_HEADS = 8
HEAD_SIZE = 128
BLOCK_TOKENS = 128
GROUP = QUERY_HEADS // KEY_VALUE_HEADS
AXES = ("seq", "head")
CHUNKS = (2, 2, 2, 2)
ROW_HEADS = 2
TILE_SLOTS = 2
STEP_BLOCKS = 2
MASKED = -1e30
SCALE = math.log2(math.e) / math.sqrt(HEAD_SIZE)
LEAST_SUM = 1e-25
GREATEST_SUM = 1e30


def attend_kernel(levels, blocks, parts, sources, place_ref, pattern_ref, keep_ref, q_ref, *refs):
    count = len(sources)
    k_refs, v_refs = refs[:count], refs[count : 2 * count]
    out_ref, token_ref = refs[-2:]
    first = place_ref[0] * blocks

    def pick(source, local):
        local = jnp.clip(local, 0, blocks - 1)
        rows = pl.ds(pl.multiple_of(local * BLOCK_TOKENS, BLOCK_TOKENS), BLOCK_TOKENS)
        return k_refs[source][rows, :], v_refs[source][rows, :]

    def gather(block):
        k_part, v_part = pick(0, block)
        ones = jnp.ones_like(v_part)
        k_parts, v_parts, lives = [k_part], [jnp.concatenate([v_part, ones], 1)], []
        for level in range(levels):
            span = 2**level
            named = pattern_ref[first + block, level]
            if span < blocks:
                local = named - first
                near_k, near_v = pick(0, local)
                far_k, far_v = pick(sources.index(1), local + blocks)
                k_part = jnp.where(local >= 0, near_k, far_k)
                v_part = jnp.where(local >= 0, near_v, far_v)
            else:
                shift = span // blocks
                k_part, v_part = pick(sources.index(shift), named - first + shift * blocks)
            live = keep_ref[first + block, level] > 0
            factor = jnp.where(live, 1.0, 0.0).astype(jnp.bfloat16)
            k_parts.append(k_part * factor)
            v_parts.append(jnp.concatenate([v_part * factor, ones * factor], 1))
            lives.append(live)
        return jnp.concatenate(k_parts, 0), jnp.concatenate(v_parts, 0), lives

    def query_rows(part, heads):
        rows = slice(part * BLOCK_TOKENS, (part + 1) * BLOCK_TOKENS)
        return jnp.concatenate(
            [q_ref[rows, h * HEAD_SIZE : (h + 1) * HEAD_SIZE] for h in heads], 0
        )

    def score(q, k):
        return lax.dot_general(
            q, k, (((1,), (1,)), ((), ())), preferred_element_type=jnp.float32
        )

    def store(part, heads, sums):
        total = sums[:, HEAD_SIZE:]
        inverse = pl.reciprocal(total, approx=True)
        inverse = inverse * (2.0 - total * inverse)
        result = (sums[:, :HEAD_SIZE] * inverse).astype(jnp.bfloat16)
        rows = slice(part * BLOCK_TOKENS, (part + 1) * BLOCK_TOKENS)
        for at, h in enumerate(heads):
            out_ref[rows, h * HEAD_SIZE : (h + 1) * HEAD_SIZE] = result[
                at * BLOCK_TOKENS : (at + 1) * BLOCK_TOKENS
            ]

    def causal_of(heads):
        shape = (heads * BLOCK_TOKENS, BLOCK_TOKENS)
        token = lax.broadcasted_iota(jnp.int32, shape, 0) % BLOCK_TOKENS
        return token >= lax.broadcasted_iota(jnp.int32, shape, 1)

    here = pl.program_id(1) * parts

    def quick():
        gathered = [gather(here + part) for part in range(parts)]
        steps = [
            (part, range(h, h + ROW_HEADS))
            for part in range(parts)
            for h in range(0, GROUP, ROW_HEADS)
        ]
        causal = causal_of(ROW_HEADS)

        count_of = levels + 1
        tiles = [
            slice(t * BLOCK_TOKENS, min(t + TILE_SLOTS, count_of) * BLOCK_TOKENS)
            for t in range(0, count_of, TILE_SLOTS)
        ]
        least = jnp.full((8, HEAD_SIZE), GREATEST_SUM, jnp.float32)
        greatest = jnp.full((8, HEAD_SIZE), LEAST_SUM, jnp.float32)
        pieces = [(part, heads, t) for part, heads in steps for t in range(len(tiles))]

        def scores_of(piece):
            part, heads, t = piece
            return score(query_rows(part, heads), gathered[part][0][tiles[t]])

        def weights_of(piece, scores):
            weights = jnp.exp2(scores * SCALE)
            if piece[2] == 0:
                diag = jnp.where(causal, weights[:, :BLOCK_TOKENS], 0.0)
                weights = jnp.concatenate([diag, weights[:, BLOCK_TOKENS:]], 1)
            return weights.astype(jnp.bfloat16)

        def product_of(piece, weights):
            part, _, t = piece
            return jnp.dot(weights, gathered[part][1][tiles[t]], preferred_element_type=jnp.float32)

        ahead = [scores_of(piece) for piece in pieces[:2]]
        behind, sums = None, None
        for at in range(len(pieces) + 1):
            if at + 2 < len(pieces):
                ahead.append(scores_of(pieces[at + 2]))
            weights = None
            if at < len(pieces):
                weights = weights_of(pieces[at], ahead.pop(0))
            if behind is not None:
                part, heads, t = pieces[at - 1]
                product = product_of(pieces[at - 1], behind)
                sums = product if t == 0 else sums + product
                if t == len(tiles) - 1:
                    store(part, heads, sums)
                    total = sums[:, HEAD_SIZE:].reshape(-1, 8, HEAD_SIZE)
                    least = jnp.minimum(least, jnp.min(total, axis=0))
                    greatest = jnp.maximum(greatest, jnp.max(total, axis=0))
            behind = weights
        return least, greatest

    def careful():
        for part in range(parts):
            k, v, lives = gather(here + part)
            bias = jnp.concatenate(
                [
                    jnp.full((1, BLOCK_TOKENS), jnp.where(live, 0.0, MASKED), jnp.float32)
                    for live in lives
                ],
                1,
            )
            causal = causal_of(1)
            for h in range(GROUP):
                scores = score(query_rows(part, [h]), k)
                diag = jnp.where(causal, scores[:, :BLOCK_TOKENS], MASKED)
                scores = jnp.concatenate([diag, scores[:, BLOCK_TOKENS:] + bias], 1)
                peak = jnp.max(scores, axis=1, keepdims=True)
                weights = jnp.exp2((scores - peak) * SCALE).astype(jnp.bfloat16)
                store(part, [h], jnp.dot(weights, v, preferred_element_type=jnp.float32))

    token_ref[0] = 0
    least, greatest = quick()
    fine = (jnp.min(least) > LEAST_SUM) & (jnp.max(greatest) < GREATEST_SUM)
    pl.when(jnp.logical_not(fine))(careful)


def attend_chunk(queries, held, sources, place, pattern, keep, first_head, heads, total, out, waited):
    rows, width = queries.shape
    blocks = rows // BLOCK_TOKENS
    levels = (blocks * total - 1).bit_length()
    group_width = GROUP * HEAD_SIZE

    parts = math.gcd(blocks, STEP_BLOCKS)
    q_block = (parts * BLOCK_TOKENS, group_width)

    def q_index(head, step, *_):
        return step, first_head + head

    in_specs = [pl.BlockSpec(q_block, q_index)]
    operands = [queries]
    for offset in (0, heads):
        for source in sources:
            array, column = held[source]
            in_specs.append(
                pl.BlockSpec(
                    (rows, HEAD_SIZE), lambda head, step, *_, o=column + offset: (0, o + head)
                )
            )
            operands.append(array)
    for array in waited:
        in_specs.append(pl.BlockSpec(memory_space=pl.ANY))
        operands.append(array)
    aliases = {}
    if out is not None:
        in_specs.append(pl.BlockSpec(memory_space=pl.ANY))
        aliases = {3 + len(operands): 0}
        operands.append(out)
    return pl.pallas_call(
        functools.partial(attend_kernel, levels, blocks, parts, sources),
        grid_spec=pltpu.PrefetchScalarGridSpec(
            num_scalar_prefetch=3,
            grid=(heads, blocks // parts),
            in_specs=in_specs,
            out_specs=[
                pl.BlockSpec(q_block, q_index),
                pl.BlockSpec(memory_space=pltpu.SMEM),
            ],
        ),
        out_shape=[
            jax.ShapeDtypeStruct((rows, width), jnp.bfloat16),
            jax.ShapeDtypeStruct((1,), jnp.int32),
        ],
        input_output_aliases=aliases,
        compiler_params=pltpu.CompilerParams(vmem_limit_bytes=44 * 2**20),
        cost_estimate=pl.CostEstimate(
            flops=5000000000,
            bytes_accessed=1,
            transcendentals=1,
        ),
    )(place, pattern, keep, *operands)


def body(queries, keys, values, pattern, keep):
    total = lax.axis_size(AXES)
    place = lax.axis_index(AXES).astype(jnp.int32)
    sources = tuple([0] + [2**b for b in range(total.bit_length() - 1)])
    stride = max(total // 4, 1)
    up = [(p, p + stride) for p in range(total - stride)]
    chunks = range(len(CHUNKS))
    distances = [stride >> k for k in range(1, stride.bit_length() - 1)]
    nearest = distances[-1]
    firsts = [sum(CHUNKS[:c]) for c in chunks]
    held = []
    for first, heads in zip(firsts, CHUNKS):
        columns = slice(first * HEAD_SIZE, (first + heads) * HEAD_SIZE)
        kv = jnp.concatenate([keys[:, columns], values[:, columns]], 1)
        held.append({0: (lax.optimization_barrier(kv), 0)})

    def part_of(chunk, source):
        array, column = held[chunk][source]
        width = 2 * CHUNKS[chunk] * HEAD_SIZE
        return array[:, column * HEAD_SIZE : column * HEAD_SIZE + width]

    def climb(*moves):
        sent = jnp.concatenate([part_of(*move) for move in moves], 1)
        arrived, column = lax.ppermute(sent, AXES, up), 0
        for chunk, source in moves:
            held[chunk][source + stride] = arrived, column
            column += 2 * CHUNKS[chunk]

    def swap(chunk, distance, token=None, other=None):
        upper = (place & distance) > (0 if token is None else token[0])
        sent = jnp.where(upper, part_of(chunk, 2 * distance), part_of(chunk, 0))
        if other is not None:
            sent = jnp.where(other != other, other, sent)
        pairs = [(p, p ^ distance) for p in range(total)]
        held[chunk][distance] = lax.ppermute(sent, AXES, pairs), 0
        if distance == 2:
            sent = jnp.where((place & 1) > 0, sent, part_of(chunk, 0))
            pairs = [(p, p ^ (3 if p & 1 else 1)) for p in range(total)]
            held[chunk][1] = lax.ppermute(sent, AXES, pairs), 0

    state = [None, None]

    def attend(chunk, *waited):
        state[:] = attend_chunk(
            queries,
            held[chunk],
            sources,
            place.reshape(1),
            pattern,
            keep,
            firsts[chunk],
            CHUNKS[chunk],
            total,
            state[0],
            waited,
        )

    climb((0, 0))
    climb((1, 0))
    climb((2, 0), (0, stride))
    climb((3, 0), (1, stride))
    climb((2, stride))
    climb((3, stride))
    for chunk in (0, 1):
        for distance in distances:
            swap(chunk, distance)
    attend(0)
    token = state[1]
    for distance in distances:
        swap(2, distance, token if distance == nearest else None)
    attend(1)
    for distance in distances:
        if distance == distances[0]:
            swap(3, distance, token)
        else:
            swap(3, distance, state[1], part_of(2, 2 * stride))
    attend(2)
    attend(3)
    return state[0]


def solution(mesh):
    return jax.shard_map(
        body,
        mesh=mesh,
        in_specs=(P(AXES, None), P(AXES, None), P(AXES, None), P(), P()),
        out_specs=P(AXES, None),
        check_vma=False,
    )
```

```python
import functools
import math

import jax
import jax.numpy as jnp
from jax import lax
from jax.experimental import pallas as pl
from jax.experimental.pallas import tpu as pltpu
from jax.sharding import PartitionSpec as P

QUERY_HEADS = 64
KEY_VALUE_HEADS = 8
HEAD_SIZE = 128
BLOCK_TOKENS = 128
GROUP = QUERY_HEADS // KEY_VALUE_HEADS
AXES = ("seq", "head")
CHUNKS = (2, 3, 2, 1)
ROW_HEADS = 2
TILE_SLOTS = 2
STEP_BLOCKS = 2
MASKED = -1e30
SCALE = math.log2(math.e) / math.sqrt(HEAD_SIZE)
LEAST_SUM = 1e-25
GREATEST_SUM = 1e30


def attend_kernel(levels, blocks, parts, sources, place_ref, pattern_ref, keep_ref, q_ref, *refs):
    count = len(sources)
    k_refs, v_refs = refs[:count], refs[count : 2 * count]
    out_ref, token_ref = refs[-2:]
    first = place_ref[0] * blocks

    def pick(source, local):
        local = jnp.clip(local, 0, blocks - 1)
        rows = pl.ds(pl.multiple_of(local * BLOCK_TOKENS, BLOCK_TOKENS), BLOCK_TOKENS)
        return k_refs[source][rows, :], v_refs[source][rows, :]

    def gather(block):
        k_part, v_part = pick(0, block)
        ones = jnp.ones_like(v_part)
        k_parts, v_parts, lives = [k_part], [jnp.concatenate([v_part, ones], 1)], []
        for level in range(levels):
            span = 2**level
            named = pattern_ref[first + block, level]
            if span < blocks:
                local = named - first
                near_k, near_v = pick(0, local)
                far_k, far_v = pick(sources.index(1), local + blocks)
                k_part = jnp.where(local >= 0, near_k, far_k)
                v_part = jnp.where(local >= 0, near_v, far_v)
            else:
                shift = span // blocks
                k_part, v_part = pick(sources.index(shift), named - first + shift * blocks)
            live = keep_ref[first + block, level] > 0
            factor = jnp.where(live, 1.0, 0.0).astype(jnp.bfloat16)
            k_parts.append(k_part * factor)
            v_parts.append(jnp.concatenate([v_part * factor, ones * factor], 1))
            lives.append(live)
        return jnp.concatenate(k_parts, 0), jnp.concatenate(v_parts, 0), lives

    def query_rows(part, heads):
        rows = slice(part * BLOCK_TOKENS, (part + 1) * BLOCK_TOKENS)
        return jnp.concatenate(
            [q_ref[rows, h * HEAD_SIZE : (h + 1) * HEAD_SIZE] for h in heads], 0
        )

    def score(q, k):
        return lax.dot_general(
            q, k, (((1,), (1,)), ((), ())), preferred_element_type=jnp.float32
        )

    def store(part, heads, sums):
        total = sums[:, HEAD_SIZE:]
        inverse = pl.reciprocal(total, approx=True)
        inverse = inverse * (2.0 - total * inverse)
        result = (sums[:, :HEAD_SIZE] * inverse).astype(jnp.bfloat16)
        rows = slice(part * BLOCK_TOKENS, (part + 1) * BLOCK_TOKENS)
        for at, h in enumerate(heads):
            out_ref[rows, h * HEAD_SIZE : (h + 1) * HEAD_SIZE] = result[
                at * BLOCK_TOKENS : (at + 1) * BLOCK_TOKENS
            ]

    def causal_of(heads):
        shape = (heads * BLOCK_TOKENS, BLOCK_TOKENS)
        token = lax.broadcasted_iota(jnp.int32, shape, 0) % BLOCK_TOKENS
        return token >= lax.broadcasted_iota(jnp.int32, shape, 1)

    here = pl.program_id(1) * parts

    def quick():
        gathered = [gather(here + part) for part in range(parts)]
        steps = [
            (part, range(h, h + ROW_HEADS))
            for part in range(parts)
            for h in range(0, GROUP, ROW_HEADS)
        ]
        causal = causal_of(ROW_HEADS)

        count_of = levels + 1
        tiles = [
            slice(t * BLOCK_TOKENS, min(t + TILE_SLOTS, count_of) * BLOCK_TOKENS)
            for t in range(0, count_of, TILE_SLOTS)
        ]
        least = jnp.full((8, HEAD_SIZE), GREATEST_SUM, jnp.float32)
        greatest = jnp.full((8, HEAD_SIZE), LEAST_SUM, jnp.float32)
        pieces = [(part, heads, t) for part, heads in steps for t in range(len(tiles))]

        def scores_of(piece):
            part, heads, t = piece
            return score(query_rows(part, heads), gathered[part][0][tiles[t]])

        def weights_of(piece, scores):
            weights = jnp.exp2(scores * SCALE)
            if piece[2] == 0:
                diag = jnp.where(causal, weights[:, :BLOCK_TOKENS], 0.0)
                weights = jnp.concatenate([diag, weights[:, BLOCK_TOKENS:]], 1)
            return weights.astype(jnp.bfloat16)

        def product_of(piece, weights):
            part, _, t = piece
            return jnp.dot(weights, gathered[part][1][tiles[t]], preferred_element_type=jnp.float32)

        ahead = [scores_of(piece) for piece in pieces[:2]]
        behind, sums = None, None
        for at in range(len(pieces) + 1):
            if at + 2 < len(pieces):
                ahead.append(scores_of(pieces[at + 2]))
            weights = None
            if at < len(pieces):
                weights = weights_of(pieces[at], ahead.pop(0))
            if behind is not None:
                part, heads, t = pieces[at - 1]
                product = product_of(pieces[at - 1], behind)
                sums = product if t == 0 else sums + product
                if t == len(tiles) - 1:
                    store(part, heads, sums)
                    total = sums[:, HEAD_SIZE:].reshape(-1, 8, HEAD_SIZE)
                    least = jnp.minimum(least, jnp.min(total, axis=0))
                    greatest = jnp.maximum(greatest, jnp.max(total, axis=0))
            behind = weights
        return least, greatest

    def careful():
        for part in range(parts):
            k, v, lives = gather(here + part)
            bias = jnp.concatenate(
                [
                    jnp.full((1, BLOCK_TOKENS), jnp.where(live, 0.0, MASKED), jnp.float32)
                    for live in lives
                ],
                1,
            )
            causal = causal_of(1)
            for h in range(GROUP):
                scores = score(query_rows(part, [h]), k)
                diag = jnp.where(causal, scores[:, :BLOCK_TOKENS], MASKED)
                scores = jnp.concatenate([diag, scores[:, BLOCK_TOKENS:] + bias], 1)
                peak = jnp.max(scores, axis=1, keepdims=True)
                weights = jnp.exp2((scores - peak) * SCALE).astype(jnp.bfloat16)
                store(part, [h], jnp.dot(weights, v, preferred_element_type=jnp.float32))

    token_ref[0] = 0
    least, greatest = quick()
    fine = (jnp.min(least) > LEAST_SUM) & (jnp.max(greatest) < GREATEST_SUM)
    pl.when(jnp.logical_not(fine))(careful)


def attend_chunk(queries, held, sources, place, pattern, keep, first_head, heads, total, out, waited):
    rows, width = queries.shape
    blocks = rows // BLOCK_TOKENS
    levels = (blocks * total - 1).bit_length()
    group_width = GROUP * HEAD_SIZE

    parts = math.gcd(blocks, STEP_BLOCKS)
    q_block = (parts * BLOCK_TOKENS, group_width)

    def q_index(head, step, *_):
        return step, first_head + head

    in_specs = [pl.BlockSpec(q_block, q_index)]
    operands = [queries]
    for offset in (0, heads):
        for source in sources:
            array, column = held[source]
            in_specs.append(
                pl.BlockSpec(
                    (rows, HEAD_SIZE), lambda head, step, *_, o=column + offset: (0, o + head)
                )
            )
            operands.append(array)
    for array in waited:
        in_specs.append(pl.BlockSpec(memory_space=pl.ANY))
        operands.append(array)
    aliases = {}
    if out is not None:
        in_specs.append(pl.BlockSpec(memory_space=pl.ANY))
        aliases = {3 + len(operands): 0}
        operands.append(out)
    return pl.pallas_call(
        functools.partial(attend_kernel, levels, blocks, parts, sources),
        grid_spec=pltpu.PrefetchScalarGridSpec(
            num_scalar_prefetch=3,
            grid=(heads, blocks // parts),
            in_specs=in_specs,
            out_specs=[
                pl.BlockSpec(q_block, q_index),
                pl.BlockSpec(memory_space=pltpu.SMEM),
            ],
        ),
        out_shape=[
            jax.ShapeDtypeStruct((rows, width), jnp.bfloat16),
            jax.ShapeDtypeStruct((1,), jnp.int32),
        ],
        input_output_aliases=aliases,
        compiler_params=pltpu.CompilerParams(vmem_limit_bytes=44 * 2**20),
        cost_estimate=pl.CostEstimate(
            flops=5000000000,
            bytes_accessed=1,
            transcendentals=1,
        ),
    )(place, pattern, keep, *operands)


def body(queries, keys, values, pattern, keep):
    total = lax.axis_size(AXES)
    place = lax.axis_index(AXES).astype(jnp.int32)
    sources = tuple([0] + [2**b for b in range(total.bit_length() - 1)])
    stride = max(total // 4, 1)
    up = [(p, p + stride) for p in range(total - stride)]
    chunks = range(len(CHUNKS))
    distances = [stride >> k for k in range(1, stride.bit_length() - 1)]
    nearest = distances[-1]
    firsts = [sum(CHUNKS[:c]) for c in chunks]
    held = []
    for first, heads in zip(firsts, CHUNKS):
        columns = slice(first * HEAD_SIZE, (first + heads) * HEAD_SIZE)
        kv = jnp.concatenate([keys[:, columns], values[:, columns]], 1)
        held.append({0: (lax.optimization_barrier(kv), 0)})

    def part_of(chunk, source):
        array, column = held[chunk][source]
        width = 2 * CHUNKS[chunk] * HEAD_SIZE
        return array[:, column * HEAD_SIZE : column * HEAD_SIZE + width]

    def climb(*moves):
        sent = jnp.concatenate([part_of(*move) for move in moves], 1)
        arrived, column = lax.ppermute(sent, AXES, up), 0
        for chunk, source in moves:
            held[chunk][source + stride] = arrived, column
            column += 2 * CHUNKS[chunk]

    def swap(chunk, distance, token=None, other=None):
        upper = (place & distance) > (0 if token is None else token[0])
        sent = jnp.where(upper, part_of(chunk, 2 * distance), part_of(chunk, 0))
        if other is not None:
            other = other[:, : sent.shape[1]]
            sent = jnp.where(other != other, other, sent)
        pairs = [(p, p ^ distance) for p in range(total)]
        held[chunk][distance] = lax.ppermute(sent, AXES, pairs), 0
        if distance == 2:
            sent = jnp.where((place & 1) > 0, sent, part_of(chunk, 0))
            pairs = [(p, p ^ (3 if p & 1 else 1)) for p in range(total)]
            held[chunk][1] = lax.ppermute(sent, AXES, pairs), 0

    state = [None, None]

    def attend(chunk, *waited):
        state[:] = attend_chunk(
            queries,
            held[chunk],
            sources,
            place.reshape(1),
            pattern,
            keep,
            firsts[chunk],
            CHUNKS[chunk],
            total,
            state[0],
            waited,
        )

    climb((0, 0))
    climb((1, 0))
    climb((2, 0), (0, stride))
    climb((3, 0), (1, stride))
    climb((2, stride))
    climb((3, stride))
    for chunk in (0, 1):
        for distance in distances:
            swap(chunk, distance)
    attend(0)
    token = state[1]
    for distance in distances:
        swap(2, distance, token if distance == nearest else None)
    attend(1)
    for distance in distances:
        if distance == distances[0]:
            swap(3, distance, token)
        else:
            swap(3, distance, state[1], part_of(2, 2 * stride))
    attend(2)
    attend(3)
    return state[0]


def solution(mesh):
    return jax.shard_map(
        body,
        mesh=mesh,
        in_specs=(P(AXES, None), P(AXES, None), P(AXES, None), P(), P()),
        out_specs=P(AXES, None),
        check_vma=False,
    )
```

```python
import functools
import math

import jax
import jax.numpy as jnp
from jax import lax
from jax.experimental import pallas as pl
from jax.experimental.pallas import tpu as pltpu
from jax.sharding import PartitionSpec as P

QUERY_HEADS = 64
KEY_VALUE_HEADS = 8
HEAD_SIZE = 128
BLOCK_TOKENS = 128
GROUP = QUERY_HEADS // KEY_VALUE_HEADS
AXES = ("seq", "head")
CHUNKS = (2, 2, 2, 2)
ROW_HEADS = 2
TILE_SLOTS = 2
STEP_BLOCKS = 2
MASKED = -1e30
SCALE = math.log2(math.e) / math.sqrt(HEAD_SIZE)
LEAST_SUM = 1e-25
GREATEST_SUM = 1e30


def attend_kernel(levels, blocks, parts, sources, place_ref, table_ref, q_ref, *refs):
    count = len(sources)
    k_refs, v_refs = refs[:count], refs[count : 2 * count]
    out_ref, token_ref = refs[-2:]
    first = place_ref[0] * blocks

    def pick(source, local):
        local = jnp.clip(local, 0, blocks - 1)
        rows = pl.ds(pl.multiple_of(local * BLOCK_TOKENS, BLOCK_TOKENS), BLOCK_TOKENS)
        return k_refs[source][rows, :], v_refs[source][rows, :]

    def gather(block):
        k_part, v_part = pick(0, block)
        ones = jnp.ones_like(v_part)
        k_parts, v_parts, lives = [k_part], [jnp.concatenate([v_part, ones], 1)], []
        for level in range(levels):
            span = 2**level
            named = table_ref[block * levels + level]
            if span < blocks:
                local = named - first
                near_k, near_v = pick(0, local)
                far_k, far_v = pick(sources.index(1), local + blocks)
                k_part = jnp.where(local >= 0, near_k, far_k)
                v_part = jnp.where(local >= 0, near_v, far_v)
            else:
                shift = span // blocks
                k_part, v_part = pick(sources.index(shift), named - first + shift * blocks)
            live = table_ref[(blocks + block) * levels + level] > 0
            factor = jnp.where(live, 1.0, 0.0).astype(jnp.bfloat16)
            k_parts.append(k_part * factor)
            v_parts.append(jnp.concatenate([v_part * factor, ones * factor], 1))
            lives.append(live)
        return jnp.concatenate(k_parts, 0), jnp.concatenate(v_parts, 0), lives

    def query_rows(part, heads):
        rows = slice(part * BLOCK_TOKENS, (part + 1) * BLOCK_TOKENS)
        return jnp.concatenate(
            [q_ref[rows, h * HEAD_SIZE : (h + 1) * HEAD_SIZE] for h in heads], 0
        )

    def score(q, k):
        return lax.dot_general(
            q, k, (((1,), (1,)), ((), ())), preferred_element_type=jnp.float32
        )

    def store(part, heads, sums):
        total = sums[:, HEAD_SIZE:]
        inverse = pl.reciprocal(total, approx=True)
        inverse = inverse * (2.0 - total * inverse)
        result = (sums[:, :HEAD_SIZE] * inverse).astype(jnp.bfloat16)
        rows = slice(part * BLOCK_TOKENS, (part + 1) * BLOCK_TOKENS)
        for at, h in enumerate(heads):
            out_ref[rows, h * HEAD_SIZE : (h + 1) * HEAD_SIZE] = result[
                at * BLOCK_TOKENS : (at + 1) * BLOCK_TOKENS
            ]

    def causal_of(heads):
        shape = (heads * BLOCK_TOKENS, BLOCK_TOKENS)
        token = lax.broadcasted_iota(jnp.int32, shape, 0) % BLOCK_TOKENS
        return token >= lax.broadcasted_iota(jnp.int32, shape, 1)

    here = pl.program_id(1) * parts

    def quick():
        gathered = [gather(here + part) for part in range(parts)]
        steps = [
            (part, range(h, h + ROW_HEADS))
            for part in range(parts)
            for h in range(0, GROUP, ROW_HEADS)
        ]
        causal = causal_of(ROW_HEADS)

        count_of = levels + 1
        tiles = [
            slice(t * BLOCK_TOKENS, min(t + TILE_SLOTS, count_of) * BLOCK_TOKENS)
            for t in range(0, count_of, TILE_SLOTS)
        ]
        least = jnp.full((8, HEAD_SIZE), GREATEST_SUM, jnp.float32)
        greatest = jnp.full((8, HEAD_SIZE), LEAST_SUM, jnp.float32)
        pieces = [(part, heads, t) for part, heads in steps for t in range(len(tiles))]

        def scores_of(piece):
            part, heads, t = piece
            return score(query_rows(part, heads), gathered[part][0][tiles[t]])

        def weights_of(piece, scores):
            weights = jnp.exp2(scores * SCALE)
            if piece[2] == 0:
                diag = jnp.where(causal, weights[:, :BLOCK_TOKENS], 0.0)
                weights = jnp.concatenate([diag, weights[:, BLOCK_TOKENS:]], 1)
            return weights.astype(jnp.bfloat16)

        def product_of(piece, weights):
            part, _, t = piece
            return jnp.dot(weights, gathered[part][1][tiles[t]], preferred_element_type=jnp.float32)

        ahead = [scores_of(piece) for piece in pieces[:2]]
        behind, sums = None, None
        for at in range(len(pieces) + 1):
            if at + 2 < len(pieces):
                ahead.append(scores_of(pieces[at + 2]))
            weights = None
            if at < len(pieces):
                weights = weights_of(pieces[at], ahead.pop(0))
            if behind is not None:
                part, heads, t = pieces[at - 1]
                product = product_of(pieces[at - 1], behind)
                sums = product if t == 0 else sums + product
                if t == len(tiles) - 1:
                    store(part, heads, sums)
                    total = sums[:, HEAD_SIZE:].reshape(-1, 8, HEAD_SIZE)
                    least = jnp.minimum(least, jnp.min(total, axis=0))
                    greatest = jnp.maximum(greatest, jnp.max(total, axis=0))
            behind = weights
        return least, greatest

    def careful():
        for part in range(parts):
            k, v, lives = gather(here + part)
            bias = jnp.concatenate(
                [
                    jnp.full((1, BLOCK_TOKENS), jnp.where(live, 0.0, MASKED), jnp.float32)
                    for live in lives
                ],
                1,
            )
            causal = causal_of(1)
            for h in range(GROUP):
                scores = score(query_rows(part, [h]), k)
                diag = jnp.where(causal, scores[:, :BLOCK_TOKENS], MASKED)
                scores = jnp.concatenate([diag, scores[:, BLOCK_TOKENS:] + bias], 1)
                peak = jnp.max(scores, axis=1, keepdims=True)
                weights = jnp.exp2((scores - peak) * SCALE).astype(jnp.bfloat16)
                store(part, [h], jnp.dot(weights, v, preferred_element_type=jnp.float32))

    token_ref[0] = 0
    least, greatest = quick()
    fine = (jnp.min(least) > LEAST_SUM) & (jnp.max(greatest) < GREATEST_SUM)
    pl.when(jnp.logical_not(fine))(careful)


def attend_chunk(queries, held, sources, place, table, first_head, heads, total, out, waited):
    rows, width = queries.shape
    blocks = rows // BLOCK_TOKENS
    levels = (blocks * total - 1).bit_length()
    group_width = GROUP * HEAD_SIZE

    parts = math.gcd(blocks, STEP_BLOCKS)
    q_block = (parts * BLOCK_TOKENS, group_width)

    def q_index(head, step, *_):
        return step, first_head + head

    in_specs = [pl.BlockSpec(q_block, q_index)]
    operands = [queries]
    for offset in (0, heads):
        for source in sources:
            array, column = held[source]
            in_specs.append(
                pl.BlockSpec(
                    (rows, HEAD_SIZE), lambda head, step, *_, o=column + offset: (0, o + head)
                )
            )
            operands.append(array)
    for array in waited:
        in_specs.append(pl.BlockSpec(memory_space=pl.ANY))
        operands.append(array)
    aliases = {}
    if out is not None:
        in_specs.append(pl.BlockSpec(memory_space=pl.ANY))
        aliases = {2 + len(operands): 0}
        operands.append(out)
    return pl.pallas_call(
        functools.partial(attend_kernel, levels, blocks, parts, sources),
        grid_spec=pltpu.PrefetchScalarGridSpec(
            num_scalar_prefetch=2,
            grid=(heads, blocks // parts),
            in_specs=in_specs,
            out_specs=[
                pl.BlockSpec(q_block, q_index),
                pl.BlockSpec(memory_space=pltpu.SMEM),
            ],
        ),
        out_shape=[
            jax.ShapeDtypeStruct((rows, width), jnp.bfloat16),
            jax.ShapeDtypeStruct((1,), jnp.int32),
        ],
        input_output_aliases=aliases,
        compiler_params=pltpu.CompilerParams(vmem_limit_bytes=44 * 2**20),
        cost_estimate=pl.CostEstimate(
            flops=5000000000,
            bytes_accessed=1,
            transcendentals=1,
        ),
    )(place, table, *operands)


def body(queries, keys, values, pattern, keep):
    total = lax.axis_size(AXES)
    place = lax.axis_index(AXES).astype(jnp.int32)
    blocks = queries.shape[0] // BLOCK_TOKENS
    levels = (blocks * total - 1).bit_length()
    table = jnp.concatenate(
        [
            lax.dynamic_slice_in_dim(x, place * blocks, blocks, 0)[:, :levels].reshape(-1)
            for x in (pattern, keep)
        ]
    )
    sources = tuple([0] + [2**b for b in range(total.bit_length() - 1)])
    stride = max(total // 4, 1)
    up = [(p, p + stride) for p in range(total - stride)]
    chunks = range(len(CHUNKS))
    distances = [stride >> k for k in range(1, stride.bit_length() - 1)]
    nearest = distances[-1]
    firsts = [sum(CHUNKS[:c]) for c in chunks]
    held = []
    for first, heads in zip(firsts, CHUNKS):
        columns = slice(first * HEAD_SIZE, (first + heads) * HEAD_SIZE)
        kv = jnp.concatenate([keys[:, columns], values[:, columns]], 1)
        held.append({0: (lax.optimization_barrier(kv), 0)})

    def part_of(chunk, source):
        array, column = held[chunk][source]
        width = 2 * CHUNKS[chunk] * HEAD_SIZE
        return array[:, column * HEAD_SIZE : column * HEAD_SIZE + width]

    def climb(*moves):
        sent = jnp.concatenate([part_of(*move) for move in moves], 1)
        arrived, column = lax.ppermute(sent, AXES, up), 0
        for chunk, source in moves:
            held[chunk][source + stride] = arrived, column
            column += 2 * CHUNKS[chunk]

    def swap(chunk, distance, token=None, other=None):
        upper = (place & distance) > (0 if token is None else token[0])
        sent = jnp.where(upper, part_of(chunk, 2 * distance), part_of(chunk, 0))
        if other is not None:
            sent = jnp.where(other != other, other, sent)
        pairs = [(p, p ^ distance) for p in range(total)]
        held[chunk][distance] = lax.ppermute(sent, AXES, pairs), 0
        if distance == 2:
            sent = jnp.where((place & 1) > 0, sent, part_of(chunk, 0))
            pairs = [(p, p ^ (3 if p & 1 else 1)) for p in range(total)]
            held[chunk][1] = lax.ppermute(sent, AXES, pairs), 0

    state = [None, None]

    def attend(chunk, *waited):
        state[:] = attend_chunk(
            queries,
            held[chunk],
            sources,
            place.reshape(1),
            table,
            firsts[chunk],
            CHUNKS[chunk],
            total,
            state[0],
            waited,
        )

    climb((0, 0))
    climb((1, 0))
    climb((2, 0), (0, stride))
    climb((3, 0), (1, stride))
    climb((2, stride))
    climb((3, stride))
    for chunk in (0, 1):
        for distance in distances:
            swap(chunk, distance)
    attend(0)
    token = state[1]
    for distance in distances:
        swap(2, distance, token if distance == nearest else None)
    attend(1)
    for distance in distances:
        if distance == distances[0]:
            swap(3, distance, token)
        else:
            swap(3, distance, state[1], part_of(2, 2 * stride))
    attend(2)
    attend(3)
    return state[0]


def solution(mesh):
    return jax.shard_map(
        body,
        mesh=mesh,
        in_specs=(P(AXES, None), P(AXES, None), P(AXES, None), P(), P()),
        out_specs=P(AXES, None),
        check_vma=False,
    )
```

```python
import functools
import math

import jax
import jax.numpy as jnp
from jax import lax
from jax.experimental import pallas as pl
from jax.experimental.pallas import tpu as pltpu
from jax.sharding import PartitionSpec as P

QUERY_HEADS = 64
KEY_VALUE_HEADS = 8
HEAD_SIZE = 128
BLOCK_TOKENS = 128
GROUP = QUERY_HEADS // KEY_VALUE_HEADS
AXES = ("seq", "head")
CHUNKS = (2, 2, 2, 2)
ROW_HEADS = 2
TILE_SLOTS = 2
STEP_BLOCKS = 2
MASKED = -1e30
SCALE = math.log2(math.e) / math.sqrt(HEAD_SIZE)
LEAST_SUM = 1e-25
GREATEST_SUM = 1e30


def attend_kernel(levels, blocks, parts, sources, place_ref, table_ref, q_ref, *refs):
    count = len(sources)
    k_refs, v_refs = refs[:count], refs[count : 2 * count]
    out_ref, token_ref = refs[-2:]
    first = place_ref[0] * blocks

    def pick(source, local):
        local = jnp.clip(local, 0, blocks - 1)
        rows = pl.ds(pl.multiple_of(local * BLOCK_TOKENS, BLOCK_TOKENS), BLOCK_TOKENS)
        return k_refs[source][rows, :], v_refs[source][rows, :]

    def gather(block):
        k_part, v_part = pick(0, block)
        ones = jnp.ones_like(v_part)
        k_parts, v_parts, lives = [k_part], [jnp.concatenate([v_part, ones], 1)], []
        for level in range(levels):
            span = 2**level
            named = table_ref[block * levels + level]
            if span < blocks:
                local = named - first
                near_k, near_v = pick(0, local)
                far_k, far_v = pick(sources.index(1), local + blocks)
                k_part = jnp.where(local >= 0, near_k, far_k)
                v_part = jnp.where(local >= 0, near_v, far_v)
            else:
                shift = span // blocks
                k_part, v_part = pick(sources.index(shift), named - first + shift * blocks)
            live = table_ref[(blocks + block) * levels + level] > 0
            factor = jnp.where(live, 1.0, 0.0).astype(jnp.bfloat16)
            k_parts.append(k_part * factor)
            v_parts.append(jnp.concatenate([v_part * factor, ones * factor], 1))
            lives.append(live)
        return jnp.concatenate(k_parts, 0), jnp.concatenate(v_parts, 0), lives

    def query_rows(part, heads):
        rows = slice(part * BLOCK_TOKENS, (part + 1) * BLOCK_TOKENS)
        return jnp.concatenate(
            [q_ref[rows, h * HEAD_SIZE : (h + 1) * HEAD_SIZE] for h in heads], 0
        )

    def score(q, k):
        return lax.dot_general(
            q, k, (((1,), (1,)), ((), ())), preferred_element_type=jnp.float32
        )

    def store(part, heads, sums):
        total = sums[:, HEAD_SIZE:]
        inverse = pl.reciprocal(total, approx=True)
        inverse = inverse * (2.0 - total * inverse)
        result = (sums[:, :HEAD_SIZE] * inverse).astype(jnp.bfloat16)
        rows = slice(part * BLOCK_TOKENS, (part + 1) * BLOCK_TOKENS)
        for at, h in enumerate(heads):
            out_ref[rows, h * HEAD_SIZE : (h + 1) * HEAD_SIZE] = result[
                at * BLOCK_TOKENS : (at + 1) * BLOCK_TOKENS
            ]

    def causal_of(heads):
        shape = (heads * BLOCK_TOKENS, BLOCK_TOKENS)
        token = lax.broadcasted_iota(jnp.int32, shape, 0) % BLOCK_TOKENS
        return token >= lax.broadcasted_iota(jnp.int32, shape, 1)

    here = pl.program_id(1) * parts

    def quick():
        gathered = [gather(here + part) for part in range(parts)]
        steps = [
            (part, range(h, h + ROW_HEADS))
            for part in range(parts)
            for h in range(0, GROUP, ROW_HEADS)
        ]
        causal = causal_of(ROW_HEADS)

        count_of = levels + 1
        tiles = [
            slice(t * BLOCK_TOKENS, min(t + TILE_SLOTS, count_of) * BLOCK_TOKENS)
            for t in range(0, count_of, TILE_SLOTS)
        ]
        least = jnp.full((8, HEAD_SIZE), GREATEST_SUM, jnp.float32)
        greatest = jnp.full((8, HEAD_SIZE), LEAST_SUM, jnp.float32)
        pieces = [(part, heads, t) for part, heads in steps for t in range(len(tiles))]

        def scores_of(piece):
            part, heads, t = piece
            return score(query_rows(part, heads), gathered[part][0][tiles[t]])

        def weights_of(piece, scores):
            weights = jnp.exp2(scores * SCALE)
            if piece[2] == 0:
                diag = jnp.where(causal, weights[:, :BLOCK_TOKENS], 0.0)
                weights = jnp.concatenate([diag, weights[:, BLOCK_TOKENS:]], 1)
            return weights.astype(jnp.bfloat16)

        def product_of(piece, weights):
            part, _, t = piece
            return jnp.dot(weights, gathered[part][1][tiles[t]], preferred_element_type=jnp.float32)

        ahead = [scores_of(piece) for piece in pieces[:2]]
        behind, sums = None, None
        for at in range(len(pieces) + 1):
            if at + 2 < len(pieces):
                ahead.append(scores_of(pieces[at + 2]))
            weights = None
            if at < len(pieces):
                weights = weights_of(pieces[at], ahead.pop(0))
            if behind is not None:
                part, heads, t = pieces[at - 1]
                product = product_of(pieces[at - 1], behind)
                sums = product if t == 0 else sums + product
                if t == len(tiles) - 1:
                    store(part, heads, sums)
                    total = sums[:, HEAD_SIZE:].reshape(-1, 8, HEAD_SIZE)
                    least = jnp.minimum(least, jnp.min(total, axis=0))
                    greatest = jnp.maximum(greatest, jnp.max(total, axis=0))
            behind = weights
        return least, greatest

    def careful():
        for part in range(parts):
            k, v, lives = gather(here + part)
            bias = jnp.concatenate(
                [
                    jnp.full((1, BLOCK_TOKENS), jnp.where(live, 0.0, MASKED), jnp.float32)
                    for live in lives
                ],
                1,
            )
            causal = causal_of(1)
            for h in range(GROUP):
                scores = score(query_rows(part, [h]), k)
                diag = jnp.where(causal, scores[:, :BLOCK_TOKENS], MASKED)
                scores = jnp.concatenate([diag, scores[:, BLOCK_TOKENS:] + bias], 1)
                peak = jnp.max(scores, axis=1, keepdims=True)
                weights = jnp.exp2((scores - peak) * SCALE).astype(jnp.bfloat16)
                store(part, [h], jnp.dot(weights, v, preferred_element_type=jnp.float32))

    token_ref[0] = 0
    least, greatest = quick()
    fine = (jnp.min(least) > LEAST_SUM) & (jnp.max(greatest) < GREATEST_SUM)
    pl.when(jnp.logical_not(fine))(careful)


def attend_chunk(queries, held, sources, place, table, first_head, heads, total, out, waited):
    rows, width = queries.shape
    blocks = rows // BLOCK_TOKENS
    levels = (blocks * total - 1).bit_length()
    group_width = GROUP * HEAD_SIZE

    parts = math.gcd(blocks, STEP_BLOCKS)
    q_block = (parts * BLOCK_TOKENS, group_width)

    def q_index(head, step, *_):
        return step, first_head + head

    in_specs = [pl.BlockSpec(q_block, q_index)]
    operands = [queries]
    for offset in (0, heads):
        for source in sources:
            array, column = held[source]
            in_specs.append(
                pl.BlockSpec(
                    (rows, HEAD_SIZE), lambda head, step, *_, o=column + offset: (0, o + head)
                )
            )
            operands.append(array)
    for array in waited:
        in_specs.append(pl.BlockSpec(memory_space=pl.ANY))
        operands.append(array)
    aliases = {}
    if out is not None:
        in_specs.append(pl.BlockSpec(memory_space=pl.ANY))
        aliases = {2 + len(operands): 0}
        operands.append(out)
    return pl.pallas_call(
        functools.partial(attend_kernel, levels, blocks, parts, sources),
        grid_spec=pltpu.PrefetchScalarGridSpec(
            num_scalar_prefetch=2,
            grid=(heads, blocks // parts),
            in_specs=in_specs,
            out_specs=[
                pl.BlockSpec(q_block, q_index),
                pl.BlockSpec(memory_space=pltpu.SMEM),
            ],
        ),
        out_shape=[
            jax.ShapeDtypeStruct((rows, width), jnp.bfloat16),
            jax.ShapeDtypeStruct((1,), jnp.int32),
        ],
        input_output_aliases=aliases,
        compiler_params=pltpu.CompilerParams(vmem_limit_bytes=44 * 2**20),
        cost_estimate=pl.CostEstimate(
            flops=5000000000,
            bytes_accessed=1,
            transcendentals=1,
        ),
    )(place, table, *operands)


def body(queries, keys, values, pattern, keep):
    total = lax.axis_size(AXES)
    place = lax.axis_index(AXES).astype(jnp.int32)
    blocks = queries.shape[0] // BLOCK_TOKENS
    levels = (blocks * total - 1).bit_length()
    table = jnp.concatenate(
        [
            lax.dynamic_slice_in_dim(x, place * blocks, blocks, 0)[:, :levels].reshape(-1)
            for x in (pattern, keep)
        ]
    )
    sources = tuple([0] + [2**b for b in range(total.bit_length() - 1)])
    stride = max(total // 4, 1)
    up = [(p, p + stride) for p in range(total - stride)]
    chunks = range(len(CHUNKS))
    distances = [stride >> k for k in range(1, stride.bit_length() - 1)]
    nearest = distances[-1]
    firsts = [sum(CHUNKS[:c]) for c in chunks]
    held = []
    for first, heads in zip(firsts, CHUNKS):
        columns = slice(first * HEAD_SIZE, (first + heads) * HEAD_SIZE)
        kv = lax.optimization_barrier(jnp.concatenate([keys[:, columns], values[:, columns]], 1))
        held.append({0: (kv, 0)})
        if first == 0:
            keys, values, _ = lax.optimization_barrier((keys, values, kv))

    def part_of(chunk, source):
        array, column = held[chunk][source]
        width = 2 * CHUNKS[chunk] * HEAD_SIZE
        return array[:, column * HEAD_SIZE : column * HEAD_SIZE + width]

    def climb(*moves):
        sent = jnp.concatenate([part_of(*move) for move in moves], 1)
        arrived, column = lax.ppermute(sent, AXES, up), 0
        for chunk, source in moves:
            held[chunk][source + stride] = arrived, column
            column += 2 * CHUNKS[chunk]

    def swap(chunk, distance, token=None, other=None):
        upper = (place & distance) > (0 if token is None else token[0])
        sent = jnp.where(upper, part_of(chunk, 2 * distance), part_of(chunk, 0))
        if other is not None:
            sent = jnp.where(other != other, other, sent)
        pairs = [(p, p ^ distance) for p in range(total)]
        held[chunk][distance] = lax.ppermute(sent, AXES, pairs), 0
        if distance == 2:
            sent = jnp.where((place & 1) > 0, sent, part_of(chunk, 0))
            pairs = [(p, p ^ (3 if p & 1 else 1)) for p in range(total)]
            held[chunk][1] = lax.ppermute(sent, AXES, pairs), 0

    state = [None, None]

    def attend(chunk, *waited):
        state[:] = attend_chunk(
            queries,
            held[chunk],
            sources,
            place.reshape(1),
            table,
            firsts[chunk],
            CHUNKS[chunk],
            total,
            state[0],
            waited,
        )

    climb((0, 0))
    climb((1, 0))
    climb((2, 0), (0, stride))
    climb((3, 0), (1, stride))
    climb((2, stride))
    climb((3, stride))
    for chunk in (0, 1):
        for distance in distances:
            swap(chunk, distance)
    attend(0)
    token = state[1]
    for distance in distances:
        swap(2, distance, token if distance == nearest else None)
    attend(1)
    for distance in distances:
        if distance == distances[0]:
            swap(3, distance, token)
        else:
            swap(3, distance, state[1], part_of(2, 2 * stride))
    attend(2)
    attend(3)
    return state[0]


def solution(mesh):
    return jax.shard_map(
        body,
        mesh=mesh,
        in_specs=(P(AXES, None), P(AXES, None), P(AXES, None), P(), P()),
        out_specs=P(AXES, None),
        check_vma=False,
    )
```
